512 devices in a mesh: tm: 16 (over z_lo, y), space: 32 (over x, z_hi, core).
Axes of the slice: x: 4, y: 4, z: 16 (z_hi: 4, z_lo: 4; z = z_hi * 4 + z_lo), core: 2. Of those that a mesh axis runs over, the one named last changes fastest.
Arguments:
- residual: float32 [4, 1024, 16384], P(None, 'tm', 'space'), may hold values from -6 to 6
- members: int32 [64, 256], P('space'), may hold values from 0 to 16383, as said below
- eig_vectors: float32 [64, 256, 256], P('space'), may hold values from -0.375 to 0.375
- eig_left: float32 [64, 256, 256], P('space'), may hold values from -0.375 to 0.375
- eig_values: float32 [64, 256], P('space'), may hold values from 0.01 to 4
- compress: float32 [64, 32, 256], P('space'), may hold values from -0.375 to 0.375
- expand: float32 [64, 256, 32], P('space'), may hold values from -1 to 1
- neighbors: int32 [64, 8], P('space'), may hold values from 0 to 63
- coupling: float32 [64, 8], P('space'), may hold values from 0.1 to 0.4
Outputs:
- correction: float32 [4, 1024, 16384], P(None, 'tm', 'space')
The draws below stay inside these ranges and needn't reach their ends.
Inputs may be any that keep to these rules, and one draw needn't show every extreme that they name: `members`: each row lists the 256 panels of one cluster and every panel appears exactly once; clusters k * 2 to (k + 1) * 2 - 1 together hold exactly the panels k * 2 * 256 to (k + 1) * 2 * 256 - 1.
All inputs are finite; a program needn't handle non-finite values.
Results may differ from the reference program's by a relative error of at most 0.0018.
Values may be sent and summed in bfloat16 or wider, within the bound.
A program may use at most 64 MiB of HBM per device.

```python
import math
import jax
import jax.numpy as jnp
from jax import lax

STEPS = 1024
PANEL = 256
RANK = 32
NEIGHBORS = 8
CL_DEV = 2
SOURCES = 4
CLUSTERS = 64
PANELS = 16384


def draw_members(key, part):
    key = jax.random.fold_in(key, 7)
    blocks = CLUSTERS // CL_DEV
    block_size = CL_DEV * PANEL
    keys = jax.random.split(key, blocks)
    shuffled = jax.vmap(lambda k: jax.random.permutation(k, block_size))(keys)
    offsets = jnp.arange(blocks).astype(jnp.int32)[:, None] * block_size
    return (shuffled.astype(jnp.int32) + offsets).reshape(CLUSTERS, PANEL)


def with_ends(array, stream_key, low, high):
    extent = array.shape
    index_at = [jax.random.randint(jax.random.fold_in(stream_key, axis), (), 0, extent[axis]) for axis in range(len(extent))]
    array = array.at[tuple(index_at)].set(low)
    longest = extent.index(max(extent))
    index_at[longest] = (index_at[longest] + 1) % extent[longest]
    return array.at[tuple(index_at)].set(high)


def block_levels(own_key, dims, cuts, smallest, top_value):
    gain, own = 1.0, jax.random.fold_in(own_key, 6)
    for dim, parts in cuts:
        heights = jnp.exp(jax.random.uniform(jax.random.fold_in(own, dim), (parts,), jnp.float32, smallest / len(cuts), top_value / len(cuts)))
        gain = gain * jnp.repeat(heights, dims[dim] // parts).reshape([-1 if axis == dim else 1 for axis in range(len(dims))])
    return gain


def centred(own_key, extent, spread, reach, cuts=(), held_as=jnp.bfloat16):
    values = jax.random.normal(own_key, extent, jnp.float32) * spread
    if len(cuts) > 0:
        values = block_levels(own_key, extent, cuts, -0.22, 0.18) * values
    return jnp.clip(values, min=-reach, max=reach).astype(held_as)


def setup_inputs(seed: int = 0) -> dict:
    key_list = jax.random.split(jax.random.key(seed), 10)
    return {
        "residual": centred(key_list[0], (SOURCES, STEPS, PANELS), 1.0, 6.0, ((1, 16), (2, 32)), jnp.float32),
        "members": draw_members(jax.random.fold_in(key_list[9], 71), 0),
        "eig_vectors": centred(key_list[2], (CLUSTERS, PANEL, PANEL), PANEL ** -0.5, 0.375, ((0, 32),), jnp.float32),
        "eig_left": centred(key_list[3], (CLUSTERS, PANEL, PANEL), PANEL ** -0.5, 0.375, ((0, 32),), jnp.float32),
        "eig_values": jnp.clip(jnp.exp(math.log(4.0) - 5.9914646 * jax.random.uniform(key_list[4], (CLUSTERS, PANEL), jnp.float32) ** block_levels(key_list[4], (CLUSTERS, PANEL), ((0, 32),), -0.2, 0.2)), 0.01, 4.0),
        "compress": centred(key_list[5], (CLUSTERS, RANK, PANEL), PANEL ** -0.5, 0.375, ((0, 32),), jnp.float32),
        "expand": centred(key_list[6], (CLUSTERS, PANEL, RANK), RANK ** -0.5, 1.0, ((0, 32),), jnp.float32),
        "neighbors": with_ends(jax.random.randint(key_list[7], (CLUSTERS, NEIGHBORS), 0, CLUSTERS), jax.random.fold_in(key_list[7], 1), 0, CLUSTERS - 1).astype(jnp.int32),
        "coupling": jnp.clip(0.1 + 0.3 * jax.random.uniform(key_list[8], (CLUSTERS, NEIGHBORS), jnp.float32) ** block_levels(key_list[8], (CLUSTERS, NEIGHBORS), ((0, 32),), -0.2, 0.2), 0.1, 0.4),
    }


def reference(residual, members, eig_vectors, eig_left, eig_values, compress, expand, neighbors, coupling):
    highest = lax.Precision.HIGHEST
    panel_order = members.reshape(-1)
    ordered = residual[:, :, panel_order]
    spectrum = jnp.fft.fft(ordered, axis=1)
    stacked = jnp.stack([jnp.real(spectrum), jnp.imag(spectrum)], 0)
    spectral = jnp.transpose(stacked.reshape(2, SOURCES, STEPS, CLUSTERS, PANEL), (3, 4, 1, 0, 2))
    in_modes = jnp.einsum("cij,cjrqk->cirqk", eig_left, spectral, precision=highest)
    phases = jnp.arange(STEPS).astype(jnp.float32) * (2.0 * math.pi / STEPS)
    shift_real = 1.0 - jnp.cos(phases)
    shift_imag = jnp.sin(phases)
    real_part = shift_real[None, None, :] + eig_values[:, :, None]
    modulus = real_part * real_part + shift_imag[None, None, :] ** 2
    gain_real = (real_part / modulus)[:, :, None, :]
    gain_imag = (-shift_imag[None, None, :] / modulus)[:, :, None, :]
    mode_real = in_modes[:, :, :, 0]
    mode_imag = in_modes[:, :, :, 1]
    scaled = jnp.stack([gain_real * mode_real - gain_imag * mode_imag,
                        gain_real * mode_imag + gain_imag * mode_real], 3)
    solved = jnp.einsum("cij,cjrqk->cirqk", eig_vectors, scaled, precision=highest)
    returned = jnp.transpose(solved, (3, 2, 4, 0, 1)).reshape(2, SOURCES, STEPS, PANELS)
    in_time = jnp.real(jnp.fft.ifft(returned[0] + 1j * returned[1], axis=1)).astype(jnp.float32)
    by_cluster = in_time.reshape(SOURCES, STEPS, CLUSTERS, PANEL)
    summary = jnp.einsum("cmj,rtcj->cmrt", compress, by_cluster, precision=highest).astype(jnp.bfloat16)
    summary = lax.optimization_barrier(summary).astype(jnp.float32)
    cluster_ids = jnp.arange(CLUSTERS).astype(jnp.int32)
    weights = jnp.sum(jnp.where(neighbors[:, :, None] == cluster_ids[None, None, :], coupling[:, :, None], 0.0), axis=1)
    mixed = jnp.einsum("cj,jmrt->cmrt", weights, summary, precision=highest)
    adjusted = jnp.einsum("cim,cmrt->rtci", expand, mixed, precision=highest).reshape(SOURCES, STEPS, PANELS)
    result = in_time - adjusted
    correction = jnp.zeros(result.shape, jnp.float32).at[:, :, panel_order].set(result)
    return correction
```

```python
import functools

import jax
import jax.numpy as jnp
from jax import lax
from jax.experimental import pallas as pl
from jax.experimental.pallas import tpu as pltpu
from jax.sharding import PartitionSpec as P

MESH = pl.DeviceIdType.MESH
RUN = 4
F32, BF16 = jnp.float32, jnp.bfloat16


def dot(a, b, dims, precision=lax.Precision.HIGHEST):
    return lax.dot_general(
        a, b, ((dims[:1], dims[1:]), ((), ())), precision=precision, preferred_element_type=F32
    )


def halves(a):
    high = a.astype(BF16)
    return high, (a - high.astype(F32)).astype(BF16)


def kernel(
    x_hbm, members_ref, v_hbm, w_hbm, lam_ref, c_hbm, e_hbm, near_ref, coup_ref, out_ref,
    x_ref, v_ref, w_ref, c_ref, e_ref, place_ref, cv_ref, ep_ref,
    ends, part_in, total_out, total_in, sum_out, sum_in, mix_out, mix_in,
    load_sem, part_send, part_recv, total_send, total_recv, sum_send, sum_recv, mix_send, mix_recv,
):
    sources, steps, panels = x_hbm.shape
    clusters, size = members_ref.shape
    rank = c_hbm.shape[1]
    rows = sources * steps
    spaces = lax.axis_size("space")
    runs = lax.axis_size("tm") // RUN
    tm, space = lax.axis_index("tm"), lax.axis_index("space")
    run, spot = tm // RUN, tm % RUN

    def run_peer(k):
        return (run * RUN + (spot + k) % RUN, space)

    def total_peer(k):
        return ((run + k) % runs * RUN + spot, space)

    def space_peer(k):
        return (tm, (space + k) % spaces)

    loads = [
        pltpu.make_async_copy(src, dst, load_sem.at[i])
        for i, (src, dst) in enumerate(
            ((x_hbm, x_ref), (w_hbm, w_ref), (v_hbm, v_ref), (c_hbm, c_ref), (e_hbm, e_ref))
        )
    ]
    for load in loads:
        load.start()

    barrier = pltpu.get_barrier_semaphore()
    for k in range(1, RUN):
        pl.semaphore_signal(barrier, inc=1, device_id=run_peer(k), device_id_type=MESH)
    for k in range(1, runs):
        pl.semaphore_signal(barrier, inc=1, device_id=total_peer(k), device_id_type=MESH)

    def greet(k, _):
        pl.semaphore_signal(barrier, inc=1, device_id=space_peer(k), device_id_type=MESH)
        return _

    lax.fori_loop(1, spaces, greet, 0)

    panel_ids = lax.broadcasted_iota(jnp.int32, (panels, size), 0) + space * panels
    for c in range(clusters):
        place_ref[c] = jnp.where(panel_ids == members_ref[c : c + 1, :], 1.0, 0.0).astype(BF16)

    lam = jnp.concatenate(
        [jnp.broadcast_to(lam_ref[c : c + 1, :], (sources, size)) for c in range(clusters)], axis=0
    )
    power = {1: 1.0 / (1.0 + lam)}
    n = 1
    while n < steps * RUN * runs:
        power[2 * n] = power[n] * power[n]
        n *= 2
    one = jnp.ones_like(lam)
    stride = [one, power[steps], power[2 * steps], power[2 * steps] * power[steps]]

    loads[0].wait()
    x_high, x_low = halves(x_ref[...].reshape(rows, panels))
    loads[1].wait()
    local = []
    for c in range(clusters):
        high = dot(x_high, place_ref[c], (1, 0), None)
        low = dot(x_low, place_ref[c], (1, 0), None)
        modes = dot(high + low, w_ref[c], (1, 1))
        own = slice(c * sources, c * sources + 1)
        first = power[1][own]
        z = (modes * first).reshape(rows // 8, 8, size)
        row = lax.broadcasted_iota(jnp.int32, (8, size), 0)
        for n in (1, 2, 4):
            z = z + jnp.where(row >= n, power[n][own], 0.0)[None] * pltpu.roll(z, n, 1)
        eight = jnp.where(row >= 4, power[4][own], 1.0) * jnp.where(row % 4 >= 2, power[2][own], 1.0)
        eight = eight * jnp.where(row % 2 >= 1, power[1][own], 1.0) * power[1][own]
        z = z.reshape(sources, steps // 8, 8, size)
        blocks = [z[:, 0]]
        for b in range(1, steps // 8):
            blocks.append(z[:, b] + eight[None] * blocks[-1][:, 7:8, :])
        local.append((blocks, eight))
        ends[c * sources : (c + 1) * sources, :] = blocks[-1][:, 7, :]

    pl.semaphore_wait(barrier, RUN - 1 + runs - 1 + spaces - 1)

    part = [
        pltpu.make_async_remote_copy(
            src_ref=ends, dst_ref=part_in.at[k - 1], send_sem=part_send.at[k - 1],
            recv_sem=part_recv.at[k - 1], device_id=run_peer(k), device_id_type=MESH,
        )
        for k in range(1, RUN)
    ]
    for copy in part:
        copy.start()

    for load in loads[2:]:
        load.wait()
    for c in range(clusters):
        cv_ref[c] = dot(c_ref[c], v_ref[c], (1, 0))
        ep_ref[c * rank : (c + 1) * rank, :] = dot(e_ref[c], place_ref[c].astype(F32), (1, 1))
    lane = lax.broadcasted_iota(jnp.int32, (1, clusters * spaces), 1)
    ids = lane % spaces * clusters + lane // spaces
    select = jnp.zeros((clusters, clusters * spaces), F32)
    for n in range(near_ref.shape[1]):
        select = select + jnp.where(near_ref[:, n : n + 1] == ids, coup_ref[:, n : n + 1], 0.0)
    select = jnp.concatenate([select[c : c + 1] for c in range(clusters)], axis=1)
    width = clusters * rows
    sum_out[:, 0, width:] = jnp.broadcast_to(select, (spaces, clusters * clusters * spaces))

    start = jnp.zeros_like(lam)
    total = jnp.zeros_like(lam)

    def stride_of(m):
        return jnp.where(m == 0, stride[0], jnp.where(m == 1, stride[1], jnp.where(m == 2, stride[2], stride[3])))

    total = ends[...] * stride_of(RUN - 1 - spot)
    for k in range(1, RUN):
        part[k - 1].wait()
        value = part_in[k - 1]
        start = start + jnp.where(spot >= k, stride[k - 1] * value, 0.0)
        total = total + stride_of(jnp.where(spot >= k, RUN - 1 - spot + k, k - 1 - spot)) * value
    total_out[...] = total
    whole = [
        pltpu.make_async_remote_copy(
            src_ref=total_out, dst_ref=total_in.at[k - 1], send_sem=total_send.at[k - 1],
            recv_sem=total_recv.at[k - 1], device_id=total_peer(k), device_id_type=MESH,
        )
        for k in range(1, runs)
    ]
    for copy in whole:
        copy.start()
    leap = power[steps * RUN]
    before = one
    carry = jnp.zeros_like(lam)
    for k in range(1, runs):
        whole[k - 1].wait()
        carry = carry + before * total_in[k - 1]
        before = before * leap
    carry = (carry + before * total) / (1.0 - power[steps * RUN * runs])
    carry = start + stride_of(spot) * carry

    solved = []
    for c in range(clusters):
        blocks, eight = local[c]
        own = slice(c * sources, (c + 1) * sources)
        step = carry[own]
        parts = []
        for b in range(steps // 8):
            parts.append(blocks[b] + eight[None] * step[:, None, :])
            step = step * power[8][own]
        y = jnp.stack(parts, axis=1).reshape(rows, size)
        solved.append(y)
        summary = dot(cv_ref[c], y, (1, 1)).astype(BF16).astype(F32)
        sum_out[:, 0, c * rows : (c + 1) * rows] = summary

    def send_sum(k, _):
        peer = space_peer(k)
        pltpu.make_async_remote_copy(
            src_ref=sum_out.at[peer[1]], dst_ref=sum_in.at[space], send_sem=sum_send,
            recv_sem=sum_recv, device_id=peer, device_id_type=MESH,
        ).start()
        return _

    lax.fori_loop(1, spaces, send_sum, 0)
    sum_in[pl.ds(space, 1)] = sum_out[pl.ds(space, 1)]

    base = None
    for c in range(clusters):
        for half in halves(dot(solved[c], v_ref[c], (1, 1))):
            term = dot(half, place_ref[c], (1, 1), None)
            base = term if base is None else base + term
    x_ref[...] = base.reshape(x_ref.shape)

    everyone = pl.ds(0, spaces - 1)
    pltpu.make_async_copy(sum_in.at[everyone], sum_in.at[everyone], sum_recv).wait()
    pltpu.make_async_copy(sum_out.at[everyone], sum_out.at[everyone], sum_send).wait()
    gathered = sum_in[...].reshape(spaces, width + clusters * clusters * spaces)
    stacked = jnp.concatenate(
        [gathered[:, c * rows : (c + 1) * rows] for c in range(clusters)], axis=0
    )
    for c in range(clusters):
        at = width + c * clusters * spaces
        mix_out[:, 0, c * rows : (c + 1) * rows] = dot(
            gathered[:, at : at + clusters * spaces], stacked, (1, 0)
        )

    def send_mix(k, _):
        peer = space_peer(k)
        pltpu.make_async_remote_copy(
            src_ref=mix_out.at[peer[1]], dst_ref=mix_in.at[space], send_sem=mix_send,
            recv_sem=mix_recv, device_id=peer, device_id_type=MESH,
        ).start()
        return _

    lax.fori_loop(1, spaces, send_mix, 0)
    mix_in[pl.ds(space, 1)] = mix_out[pl.ds(space, 1)]
    pltpu.make_async_copy(mix_in.at[everyone], mix_in.at[everyone], mix_recv).wait()
    pltpu.make_async_copy(mix_out.at[everyone], mix_out.at[everyone], mix_send).wait()

    mixed = mix_in[...].reshape(rank, width)
    mixed = jnp.concatenate([mixed[:, c * rows : (c + 1) * rows] for c in range(clusters)], axis=0)
    adjusted = dot(mixed, ep_ref[...], (0, 0))
    out_ref[...] = x_ref[...] - adjusted.reshape(out_ref.shape)


def on_device(
    residual, members, eig_vectors, eig_left, eig_values, compress, expand, neighbors, coupling
):
    sources, steps, panels = residual.shape
    clusters, size = members.shape
    rank = compress.shape[1]
    rows = sources * steps
    spaces = lax.axis_size("space")
    runs = lax.axis_size("tm") // RUN
    assert rank == spaces and steps % 8 == 0 and clusters * sources == 8
    carry = (clusters * sources, size)
    width = clusters * rows
    message = width + clusters * clusters * spaces
    anywhere, vmem = pl.BlockSpec(memory_space=pl.ANY), pl.BlockSpec(memory_space=pltpu.VMEM)
    dma = pltpu.SemaphoreType.DMA
    return pl.pallas_call(
        kernel,
        out_shape=jax.ShapeDtypeStruct(residual.shape, F32),
        in_specs=[anywhere, vmem, anywhere, anywhere, vmem, anywhere, anywhere, vmem, vmem],
        out_specs=vmem,
        scratch_shapes=[
            pltpu.VMEM(residual.shape, F32),
            pltpu.VMEM(eig_vectors.shape, F32),
            pltpu.VMEM(eig_left.shape, F32),
            pltpu.VMEM(compress.shape, F32),
            pltpu.VMEM(compress.shape, F32),
            pltpu.VMEM((clusters, panels, size), BF16),
            pltpu.VMEM((clusters, rank, size), F32),
            pltpu.VMEM((clusters * rank, panels), F32),
            pltpu.VMEM(carry, F32),
            pltpu.VMEM((RUN - 1,) + carry, F32),
            pltpu.VMEM(carry, F32),
            pltpu.VMEM((runs - 1,) + carry, F32),
            pltpu.VMEM((spaces, 1, message), F32),
            pltpu.VMEM((spaces, 1, message), F32),
            pltpu.VMEM((spaces, 1, width), F32),
            pltpu.VMEM((spaces, 1, width), F32),
            dma((5,)),
            dma((RUN - 1,)),
            dma((RUN - 1,)),
            dma((runs - 1,)),
            dma((runs - 1,)),
            dma(()),
            dma(()),
            dma(()),
            dma(()),
        ],
        compiler_params=pltpu.CompilerParams(
            collective_id=0, has_side_effects=True, vmem_limit_bytes=60 * 1024 * 1024
        ),
    )(residual, members, eig_vectors, eig_left, eig_values, compress, jnp.swapaxes(expand, 1, 2), neighbors, coupling)


def solution(mesh):
    return jax.shard_map(
        on_device,
        mesh=mesh,
        in_specs=(
            P(None, "tm", "space"),
            P("space", None),
            P("space", None, None),
            P("space", None, None),
            P("space", None),
            P("space", None, None),
            P("space", None, None),
            P("space", None),
            P("space", None),
        ),
        out_specs=P(None, "tm", "space"),
        check_vma=False,
    )
```

```python
import jax
import jax.numpy as jnp
from jax import lax
from jax.experimental import pallas as pl
from jax.experimental.pallas import tpu as pltpu
from jax.sharding import PartitionSpec as P

MESH = pl.DeviceIdType.MESH
F32, BF16 = jnp.float32, jnp.bfloat16
PLANES, CORES = 4, 2
TILE, LANES = 8, 128


def dot(a, b, dims):
    return lax.dot_general(
        a, b, ((dims[:1], dims[1:]), ((), ())), preferred_element_type=F32
    )


def halves(a):
    high = a.astype(BF16)
    return high, (a - high.astype(F32)).astype(BF16)


def dot3(a, b, dims):
    return dot(a[0], b[0], dims) + (dot(a[0], b[1], dims) + dot(a[1], b[0], dims))


def kernel(
    x_hbm, members_hbm, v_hbm, w_hbm, lam_hbm, c_hbm, e_hbm, near_hbm, coup_hbm, out_ref,
    x_ref, members_ref, v_ref, w_ref, lam_ref, c_ref, e_ref, near_ref, coup_ref,
    place_ref, cv_ref, ep_ref, base_ref,
    ends, ends_in, sel_out, sel_in, sum_out, sum_in, mix_out, mix_in,
    load_sem, answer_sem, ends_send, ends_recv, sel_send, sel_recv, sum_send, sum_recv,
    mix_send, mix_recv,
):
    sources, steps, panels = x_ref.shape
    clusters, size = members_ref.shape
    rank = c_ref.shape[1]
    rows = sources * steps
    times, spaces = lax.axis_size("tm"), lax.axis_size("space")
    near = spaces // PLANES
    tm, space = lax.axis_index("tm"), lax.axis_index("space")
    plane = space // CORES % PLANES
    spot = space // (PLANES * CORES) * CORES + space % CORES
    per_block = rank // near

    def peer(at_plane, at_spot):
        return at_spot // CORES * (PLANES * CORES) + at_plane * CORES + at_spot % CORES

    def each(low, high, act):
        def body(i, _):
            act(i)
            return _

        lax.fori_loop(low, high, body, 0)

    loads = [
        pltpu.make_async_copy(src, dst, load_sem.at[i])
        for i, (src, dst) in enumerate(
            (
                (members_hbm, members_ref),
                (x_hbm, x_ref),
                (w_hbm, w_ref),
                (lam_hbm, lam_ref),
                (v_hbm, v_ref),
                (c_hbm, c_ref),
                (e_hbm, e_ref),
                (near_hbm, near_ref),
                (coup_hbm, coup_ref),
            )
        )
    ]
    for load in loads:
        load.start()

    barrier = pltpu.get_barrier_semaphore()

    def greet(device):
        pl.semaphore_signal(barrier, inc=1, device_id=device, device_id_type=MESH)

    each((plane + 1) * near, spaces, lambda i: greet((tm, peer(i // near, i % near))))
    each(1, times, lambda k: greet(((tm + k) % times, space)))
    each(1, near, lambda k: greet((tm, peer(plane, (spot + k) % near))))

    loads[0].wait()
    panel_ids = lax.broadcasted_iota(jnp.int32, (panels, size), 0) + space * panels
    for c in range(clusters):
        place_ref[c] = jnp.where(panel_ids == members_ref[c : c + 1, :], 1.0, 0.0).astype(BF16)

    loads[1].wait()
    x = halves(x_ref[...].reshape(rows, panels))
    ordered = [[dot(half, place_ref[c], (1, 0)).astype(BF16) for half in x] for c in range(clusters)]
    loads[2].wait()
    loads[3].wait()

    lam = jnp.concatenate(
        [jnp.broadcast_to(lam_ref[c : c + 1, :], (sources, size)) for c in range(clusters)], axis=0
    )
    power = {1: 1.0 / (1.0 + lam)}
    n = 1
    while n < steps * times:
        power[2 * n] = power[n] * power[n]
        n *= 2

    local = []
    for c in range(clusters):
        modes = dot3(ordered[c], halves(w_ref[c]), (1, 1))
        own = slice(c * sources, c * sources + 1)
        z = (modes * power[1][own]).reshape(rows // TILE, TILE, size)
        row = lax.broadcasted_iota(jnp.int32, (TILE, size), 0)
        ramp = power[1][own]
        for n in (1, 2, 4):
            z = z + jnp.where(row >= n, power[n][own], 0.0)[None] * pltpu.roll(z, n, 1)
            ramp = ramp * jnp.where(row // n % 2 == 1, power[n][own], 1.0)
        z = z.reshape(sources, steps // TILE, TILE, size)
        blocks = [z[:, 0]]
        for b in range(1, steps // TILE):
            blocks.append(z[:, b] + ramp[None] * blocks[-1][:, TILE - 1 :, :])
        local.append((blocks, ramp))
        ends[c * sources : (c + 1) * sources, :] = blocks[-1][:, TILE - 1, :]

    pl.semaphore_wait(barrier, times - 1 + near - 1 + plane * near)

    def copy(src, dst, send, recv, device):
        return pltpu.make_async_remote_copy(
            src_ref=src, dst_ref=dst, send_sem=send, recv_sem=recv,
            device_id=device, device_id_type=MESH,
        )

    each(
        1, times,
        lambda k: copy(ends, ends_in.at[k - 1], ends_send, ends_recv, ((tm + k) % times, space)).start(),
    )
    each(
        0, plane * near,
        lambda i: pl.semaphore_signal(
            answer_sem, inc=1, device_id=(tm, peer(i // near, i % near)), device_id_type=MESH
        ),
    )

    for load in loads[4:]:
        load.wait()
    coupled = [
        jnp.concatenate(
            [jnp.broadcast_to(ref[c : c + 1, :], (per_block, ref.shape[1])) for c in range(clusters)],
            axis=0,
        )
        for ref in (near_ref, coup_ref)
    ]
    spread = (TILE, spaces * TILE)
    lane = lax.broadcasted_iota(jnp.int32, spread, 1)
    select = jnp.zeros(spread, F32)
    for n in range(near_ref.shape[1]):
        hit = coupled[0][:, n : n + 1] == lane // per_block
        select = select + jnp.where(hit, coupled[1][:, n : n + 1], 0.0)
    same = lane % per_block == lax.broadcasted_iota(jnp.int32, spread, 0) % per_block
    sel_out[...] = jnp.where(same, select, 0.0)
    each(
        1, near,
        lambda k: copy(
            sel_out, sel_in.at[spot], sel_send, sel_recv, (tm, peer(plane, (spot + k) % near))
        ).start(),
    )
    sel_in[pl.ds(spot, 1)] = sel_out[...][None]

    cv_ref[...] = jnp.zeros_like(cv_ref)
    vectors = [halves(v_ref[c]) for c in range(clusters)]
    for c in range(clusters):
        at = slice(c * per_block, (c + 1) * per_block)
        cv = dot3(halves(c_ref[c]), vectors[c], (1, 0))
        spread_e = [dot(half, place_ref[c], (1, 1)) for half in halves(e_ref[c])]
        ep = spread_e[0] + spread_e[1]
        for b in range(near):
            block = slice(b * per_block, (b + 1) * per_block)
            cv_ref[b, at, c * size : (c + 1) * size] = cv[block]
            ep_ref[b, at, :] = ep[block]

    others = pl.ds(0, times - 1)
    pltpu.make_async_copy(ends_in.at[others], ends_in.at[others], ends_recv).wait()
    carry = ends[...]
    for k in range(times - 1, 0, -1):
        carry = carry * power[steps] + ends_in[k - 1]
    carry = carry / (1.0 - power[steps * times])

    solved = []
    for c in range(clusters):
        blocks, ramp = local[c]
        own = slice(c * sources, (c + 1) * sources)
        step = carry[own]
        parts = []
        for b in range(steps // TILE):
            parts.append(blocks[b] + ramp[None] * step[:, None, :])
            step = step * power[TILE][own]
        solved.append(halves(jnp.stack(parts, axis=1).reshape(rows, size)))
    compress = halves(cv_ref[...].reshape(rank * clusters, panels))
    summary = None
    for c in range(clusters):
        at = slice(c * size, (c + 1) * size)
        term = dot3([half[:, at] for half in compress], solved[c], (1, 1))
        summary = term if summary is None else summary + term
    summary = summary.reshape(near, TILE, rows)
    sum_out[...] = jnp.concatenate(
        [summary[:, :, i : i + LANES] for i in range(0, rows, LANES)], axis=1
    ).astype(BF16)

    def send_sum(i):
        copy(
            sum_out.at[i % near], sum_in.at[space], sum_send, sum_recv,
            (tm, peer(i // near, i % near)),
        ).start()

    each(0, plane * near, send_sum)
    each(1, near, lambda k: send_sum(plane * near + (spot + k) % near))

    @pl.when(plane < PLANES - 1)
    def _():
        pl.semaphore_wait(answer_sem, (PLANES - 1 - plane) * near)

    each((plane + 1) * near, spaces, send_sum)
    sum_in[pl.ds(space, 1)] = sum_out[pl.ds(spot, 1)]

    base = None
    for c in range(clusters):
        for half in halves(dot3(solved[c], vectors[c], (1, 1))):
            term = dot(half, place_ref[c], (1, 1))
            base = term if base is None else base + term
    base_ref[...] = base
    expand = halves(ep_ref[...].reshape(rank * clusters, panels))

    plane_peers = pl.ds(0, near - 1)
    pltpu.make_async_copy(sel_in.at[plane_peers], sel_in.at[plane_peers], sel_recv).wait()
    selector = halves(sel_in[...].reshape(near * TILE, spaces * TILE))
    everyone = pl.ds(0, spaces - 1)
    pltpu.make_async_copy(sum_in.at[everyone], sum_in.at[everyone], sum_recv).wait()
    gathered = sum_in[...].astype(F32)
    for i in range(rows // LANES):
        part = gathered[:, i * TILE : (i + 1) * TILE, :].reshape(spaces * TILE, LANES).astype(BF16)
        mixed = dot(selector[0], part, (1, 0)) + dot(selector[1], part, (1, 0))
        mix_out[:, :, i * LANES : (i + 1) * LANES] = mixed.reshape(near, TILE, LANES)

    def send_mix(k):
        to = (spot + k) % near
        copy(mix_out.at[to], mix_in.at[spot], mix_send, mix_recv, (tm, peer(plane, to))).start()

    each(1, near, send_mix)
    mix_in[pl.ds(spot, 1)] = mix_out[pl.ds(spot, 1)]
    pltpu.make_async_copy(mix_in.at[plane_peers], mix_in.at[plane_peers], mix_recv).wait()

    mixed = halves(mix_in[...].reshape(rank * clusters, rows))
    out_ref[...] = (base_ref[...] - dot3(mixed, expand, (0, 0))).reshape(out_ref.shape)

    pltpu.make_async_copy(ends_in.at[others], ends_in.at[others], ends_send).wait()
    pltpu.make_async_copy(sel_in.at[plane_peers], sel_in.at[plane_peers], sel_send).wait()
    pltpu.make_async_copy(sum_in.at[everyone], sum_in.at[everyone], sum_send).wait()
    pltpu.make_async_copy(mix_in.at[plane_peers], mix_in.at[plane_peers], mix_send).wait()


def on_device(
    residual, members, eig_vectors, eig_left, eig_values, compress, expand, neighbors, coupling
):
    sources, steps, panels = residual.shape
    clusters, size = members.shape
    rank = compress.shape[1]
    rows = sources * steps
    times, spaces = lax.axis_size("tm"), lax.axis_size("space")
    near = spaces // PLANES
    assert clusters * sources == TILE and clusters * rank == near * TILE
    assert steps % TILE == 0 and rows == 2 * LANES and clusters * size == panels
    args = (
        residual, members, eig_vectors, eig_left, eig_values, compress,
        jnp.swapaxes(expand, 1, 2), neighbors, coupling,
    )
    carry = (clusters * sources, size)
    block = (2 * TILE, LANES)
    dma = pltpu.SemaphoreType.DMA
    return pl.pallas_call(
        kernel,
        out_shape=jax.ShapeDtypeStruct(residual.shape, F32),
        in_specs=[pl.BlockSpec(memory_space=pl.ANY)] * len(args),
        out_specs=pl.BlockSpec(memory_space=pltpu.VMEM),
        scratch_shapes=[pltpu.VMEM(a.shape, a.dtype) for a in args]
        + [
            pltpu.VMEM((clusters, panels, size), BF16),
            pltpu.VMEM((near, TILE, panels), F32),
            pltpu.VMEM((near, TILE, panels), F32),
            pltpu.VMEM((rows, panels), F32),
            pltpu.VMEM(carry, F32),
            pltpu.VMEM((times - 1,) + carry, F32),
            pltpu.VMEM((TILE, spaces * TILE), F32),
            pltpu.VMEM((near, TILE, spaces * TILE), F32),
            pltpu.VMEM((near,) + block, BF16),
            pltpu.VMEM((spaces,) + block, BF16),
            pltpu.VMEM((near, TILE, rows), F32),
            pltpu.VMEM((near, TILE, rows), F32),
            dma((len(args),)),
            pltpu.SemaphoreType.REGULAR,
        ]
        + [dma(())] * 8,
        compiler_params=pltpu.CompilerParams(
            collective_id=0, has_side_effects=True, vmem_limit_bytes=60 * 1024 * 1024
        ),
    )(*args)


def solution(mesh):
    return jax.shard_map(
        on_device,
        mesh=mesh,
        in_specs=(
            P(None, "tm", "space"),
            P("space", None),
            P("space", None, None),
            P("space", None, None),
            P("space", None),
            P("space", None, None),
            P("space", None, None),
            P("space", None),
            P("space", None),
        ),
        out_specs=P(None, "tm", "space"),
        check_vma=False,
    )
```

```python
import jax
import jax.numpy as jnp
from jax import lax
from jax.experimental import pallas as pl
from jax.experimental.pallas import tpu as pltpu
from jax.sharding import PartitionSpec as P

MESH = pl.DeviceIdType.MESH
F32, BF16 = jnp.float32, jnp.bfloat16
PLANES, CORES = 4, 2
HUB = PLANES // 2
TILE, LANES = 8, 128


def dot(a, b, dims):
    return lax.dot_general(
        a, b, ((dims[:1], dims[1:]), ((), ())), preferred_element_type=F32
    )


def halves(a):
    high = a.astype(BF16)
    return high, (a - high.astype(F32)).astype(BF16)


def dot3(a, b, dims):
    return dot(a[0], b[0], dims) + (dot(a[0], b[1], dims) + dot(a[1], b[0], dims))


def kernel(
    x_hbm, members_hbm, v_hbm, w_hbm, lam_hbm, c_hbm, e_hbm, near_hbm, coup_hbm, out_ref,
    x_ref, members_ref, v_ref, w_ref, lam_ref, c_ref, e_ref, near_ref, coup_ref,
    place_ref, cv_ref, ep_ref, base_ref,
    ends, ends_in, sel_out, sel_in, sum_out, sum_in, mix_out, mix_in,
    load_sem, answer_sem, ends_send, ends_recv, sel_send, sel_recv, sum_send, sum_recv,
    mix_send, mix_recv,
):
    sources, steps, panels = x_ref.shape
    clusters, size = members_ref.shape
    rank = c_ref.shape[1]
    rows = sources * steps
    times, spaces = lax.axis_size("tm"), lax.axis_size("space")
    near = spaces // PLANES
    tm, space = lax.axis_index("tm"), lax.axis_index("space")
    plane = space // CORES % PLANES
    spot = space // (PLANES * CORES) * CORES + space % CORES
    per_block = rank // near

    def peer(at_plane, at_spot):
        return at_spot // CORES * (PLANES * CORES) + at_plane * CORES + at_spot % CORES

    def each(low, high, act):
        if isinstance(low, int) and isinstance(high, int):
            for i in range(low, high):
                act(i)
            return

        def body(i, _):
            act(i)
            return _

        lax.fori_loop(low, high, body, 0)

    loads = [
        pltpu.make_async_copy(src, dst, load_sem.at[i])
        for i, (src, dst) in enumerate(
            (
                (members_hbm, members_ref),
                (x_hbm, x_ref),
                (w_hbm, w_ref),
                (lam_hbm, lam_ref),
                (v_hbm, v_ref),
                (c_hbm, c_ref),
                (e_hbm, e_ref),
                (near_hbm, near_ref),
                (coup_hbm, coup_ref),
            )
        )
    ]
    for load in loads:
        load.start()

    barrier = pltpu.get_barrier_semaphore()

    def greet(device):
        pl.semaphore_signal(barrier, inc=1, device_id=device, device_id_type=MESH)

    @pl.when(plane != HUB)
    def _():
        each(0, near, lambda k: greet((tm, peer(HUB, k))))

    each(1, times, lambda k: greet(((tm + k) % times, space)))
    each(1, near, lambda k: greet((tm, peer(plane, (spot + k) % near))))

    loads[0].wait()
    panel_ids = lax.broadcasted_iota(jnp.int32, (panels, size), 0) + space * panels
    for c in range(clusters):
        place_ref[c] = jnp.where(panel_ids == members_ref[c : c + 1, :], 1.0, 0.0).astype(BF16)

    loads[1].wait()
    x = halves(x_ref[...].reshape(rows, panels))
    ordered = [[dot(half, place_ref[c], (1, 0)).astype(BF16) for half in x] for c in range(clusters)]
    loads[2].wait()
    loads[3].wait()

    lam = jnp.concatenate(
        [jnp.broadcast_to(lam_ref[c : c + 1, :], (sources, size)) for c in range(clusters)], axis=0
    )
    power = {1: 1.0 / (1.0 + lam)}
    n = 1
    while n < steps * times:
        power[2 * n] = power[n] * power[n]
        n *= 2

    local = []
    for c in range(clusters):
        modes = dot3(ordered[c], halves(w_ref[c]), (1, 1))
        own = slice(c * sources, c * sources + 1)
        z = (modes * power[1][own]).reshape(rows // TILE, TILE, size)
        row = lax.broadcasted_iota(jnp.int32, (TILE, size), 0)
        ramp = power[1][own]
        for n in (1, 2, 4):
            z = z + jnp.where(row >= n, power[n][own], 0.0)[None] * pltpu.roll(z, n, 1)
            ramp = ramp * jnp.where(row // n % 2 == 1, power[n][own], 1.0)
        z = z.reshape(sources, steps // TILE, TILE, size)
        blocks = [z[:, 0]]
        for b in range(1, steps // TILE):
            blocks.append(z[:, b] + ramp[None] * blocks[-1][:, TILE - 1 :, :])
        local.append((blocks, ramp))
        ends[c * sources : (c + 1) * sources, :] = blocks[-1][:, TILE - 1, :]

    pl.semaphore_wait(barrier, times - 1 + near - 1 + jnp.where(plane == HUB, spaces - near, 0))

    def copy(src, dst, send, recv, device):
        return pltpu.make_async_remote_copy(
            src_ref=src, dst_ref=dst, send_sem=send, recv_sem=recv,
            device_id=device, device_id_type=MESH,
        )

    each(
        1, times,
        lambda k: copy(ends, ends_in.at[k - 1], ends_send, ends_recv, ((tm + k) % times, space)).start(),
    )

    @pl.when(plane == HUB)
    def _():
        for k in range(1, PLANES):
            pl.semaphore_signal(
                answer_sem, inc=1, device_id=(tm, peer((HUB + k) % PLANES, spot)), device_id_type=MESH
            )


    for load in loads[4:]:
        load.wait()
    coupled = [
        jnp.concatenate(
            [jnp.broadcast_to(ref[c : c + 1, :], (per_block, ref.shape[1])) for c in range(clusters)],
            axis=0,
        )
        for ref in (near_ref, coup_ref)
    ]
    spread = (TILE, spaces * TILE)
    lane = lax.broadcasted_iota(jnp.int32, spread, 1)
    select = jnp.zeros(spread, F32)
    for n in range(near_ref.shape[1]):
        hit = coupled[0][:, n : n + 1] == lane // per_block
        select = select + jnp.where(hit, coupled[1][:, n : n + 1], 0.0)
    same = lane % per_block == lax.broadcasted_iota(jnp.int32, spread, 0) % per_block
    sel_out[...] = jnp.where(same, select, 0.0)
    each(
        1, near,
        lambda k: copy(
            sel_out, sel_in.at[spot], sel_send, sel_recv, (tm, peer(plane, (spot + k) % near))
        ).start(),
    )
    sel_in[pl.ds(spot, 1)] = sel_out[...][None]

    cv_ref[...] = jnp.zeros_like(cv_ref)
    vectors = [halves(v_ref[c]) for c in range(clusters)]
    for c in range(clusters):
        at = slice(c * per_block, (c + 1) * per_block)
        cv = dot3(halves(c_ref[c]), vectors[c], (1, 0))
        spread_e = [dot(half, place_ref[c], (1, 1)) for half in halves(e_ref[c])]
        ep = spread_e[0] + spread_e[1]
        for b in range(near):
            block = slice(b * per_block, (b + 1) * per_block)
            cv_ref[b, at, c * size : (c + 1) * size] = cv[block]
            ep_ref[b, at, :] = ep[block]

    others = pl.ds(0, times - 1)
    pltpu.make_async_copy(ends_in.at[others], ends_in.at[others], ends_recv).wait()
    carry = ends[...]
    for k in range(times - 1, 0, -1):
        carry = carry * power[steps] + ends_in[k - 1]
    carry = carry / (1.0 - power[steps * times])

    solved = []
    for c in range(clusters):
        blocks, ramp = local[c]
        own = slice(c * sources, (c + 1) * sources)
        step = carry[own]
        parts = []
        for b in range(steps // TILE):
            parts.append(blocks[b] + ramp[None] * step[:, None, :])
            step = step * power[TILE][own]
        solved.append(halves(jnp.stack(parts, axis=1).reshape(rows, size)))
    compress = halves(cv_ref[...].reshape(rank * clusters, panels))
    summary = None
    for c in range(clusters):
        at = slice(c * size, (c + 1) * size)
        term = dot3([half[:, at] for half in compress], solved[c], (1, 1))
        summary = term if summary is None else summary + term
    summary = summary.reshape(near, TILE, rows)
    sum_out[...] = jnp.concatenate(
        [summary[:, :, i : i + LANES] for i in range(0, rows, LANES)], axis=1
    ).astype(BF16)

    def send_sum(i):
        copy(
            sum_out.at[i % near], sum_in.at[space], sum_send, sum_recv,
            (tm, peer(i // near, i % near)),
        ).start()

    @pl.when(plane != HUB)
    def _():
        pl.semaphore_wait(answer_sem, 1)

    each(0, plane * near, send_sum)
    each(1, near, lambda k: send_sum(plane * near + (spot + k) % near))
    each((plane + 1) * near, spaces, send_sum)
    sum_in[pl.ds(space, 1)] = sum_out[pl.ds(spot, 1)]

    base = None
    for c in range(clusters):
        for half in halves(dot3(solved[c], vectors[c], (1, 1))):
            term = dot(half, place_ref[c], (1, 1))
            base = term if base is None else base + term
    base_ref[...] = base
    expand = halves(-ep_ref[...].reshape(rank * clusters, panels))
    expand = jnp.concatenate([expand[0], expand[1], expand[0]], axis=0)

    plane_peers = pl.ds(0, near - 1)
    pltpu.make_async_copy(sel_in.at[plane_peers], sel_in.at[plane_peers], sel_recv).wait()
    selector = halves(sel_in[...].reshape(near * TILE, spaces * TILE))
    everyone = pl.ds(0, spaces - 1)
    pltpu.make_async_copy(sum_in.at[everyone], sum_in.at[everyone], sum_recv).wait()
    gathered = sum_in[...].astype(F32)
    for i in range(rows // LANES):
        part = gathered[:, i * TILE : (i + 1) * TILE, :].reshape(spaces * TILE, LANES).astype(BF16)
        mixed = dot(selector[0], part, (1, 0)) + dot(selector[1], part, (1, 0))
        mix_out[:, :, i * LANES : (i + 1) * LANES] = mixed.reshape(near, TILE, LANES)

    def send_mix(k):
        to = (spot + k) % near
        copy(mix_out.at[to], mix_in.at[spot], mix_send, mix_recv, (tm, peer(plane, to))).start()

    each(1, near, send_mix)
    mix_in[pl.ds(spot, 1)] = mix_out[pl.ds(spot, 1)]
    pltpu.make_async_copy(mix_in.at[plane_peers], mix_in.at[plane_peers], mix_recv).wait()

    mixed = halves(mix_in[...].reshape(rank * clusters, rows))
    mixed = jnp.concatenate([mixed[0], mixed[0], mixed[1]], axis=0)
    out_ref[...] = (base_ref[...] + dot(mixed, expand, (0, 0))).reshape(out_ref.shape)

    pltpu.make_async_copy(ends_in.at[others], ends_in.at[others], ends_send).wait()
    pltpu.make_async_copy(sel_in.at[plane_peers], sel_in.at[plane_peers], sel_send).wait()
    pltpu.make_async_copy(sum_in.at[everyone], sum_in.at[everyone], sum_send).wait()
    pltpu.make_async_copy(mix_in.at[plane_peers], mix_in.at[plane_peers], mix_send).wait()


def on_device(
    residual, members, eig_vectors, eig_left, eig_values, compress, expand, neighbors, coupling
):
    sources, steps, panels = residual.shape
    clusters, size = members.shape
    rank = compress.shape[1]
    rows = sources * steps
    times, spaces = lax.axis_size("tm"), lax.axis_size("space")
    near = spaces // PLANES
    assert clusters * sources == TILE and clusters * rank == near * TILE
    assert steps % TILE == 0 and rows == 2 * LANES and clusters * size == panels
    args = (
        residual, members, eig_vectors, eig_left, eig_values, compress,
        jnp.swapaxes(expand, 1, 2), neighbors, coupling,
    )
    carry = (clusters * sources, size)
    block = (2 * TILE, LANES)
    dma = pltpu.SemaphoreType.DMA
    return pl.pallas_call(
        kernel,
        out_shape=pltpu.VMEM(residual.shape, F32),
        in_specs=[pl.BlockSpec(memory_space=pltpu.HBM)] * len(args),
        out_specs=pl.BlockSpec(memory_space=pltpu.VMEM),
        scratch_shapes=[pltpu.VMEM(a.shape, a.dtype) for a in args]
        + [
            pltpu.VMEM((clusters, panels, size), BF16),
            pltpu.VMEM((near, TILE, panels), F32),
            pltpu.VMEM((near, TILE, panels), F32),
            pltpu.VMEM((rows, panels), F32),
            pltpu.VMEM(carry, F32),
            pltpu.VMEM((times - 1,) + carry, F32),
            pltpu.VMEM((TILE, spaces * TILE), F32),
            pltpu.VMEM((near, TILE, spaces * TILE), F32),
            pltpu.VMEM((near,) + block, BF16),
            pltpu.VMEM((spaces,) + block, BF16),
            pltpu.VMEM((near, TILE, rows), F32),
            pltpu.VMEM((near, TILE, rows), F32),
            dma((len(args),)),
            pltpu.SemaphoreType.REGULAR,
        ]
        + [dma(())] * 8,
        compiler_params=pltpu.CompilerParams(
            collective_id=0, has_side_effects=True, vmem_limit_bytes=32 * 1024 * 1024
        ),
    )(*(pltpu.with_memory_space_constraint(a, pltpu.HBM) for a in args))


def solution(mesh):
    return jax.shard_map(
        on_device,
        mesh=mesh,
        in_specs=(
            P(None, "tm", "space"),
            P("space", None),
            P("space", None, None),
            P("space", None, None),
            P("space", None),
            P("space", None, None),
            P("space", None, None),
            P("space", None),
            P("space", None),
        ),
        out_specs=P(None, "tm", "space"),
        check_vma=False,
    )
```

```python
import jax
import jax.numpy as jnp
from jax import lax
from jax.experimental import pallas as pl
from jax.experimental.pallas import tpu as pltpu
from jax.sharding import PartitionSpec as P

MESH = pl.DeviceIdType.MESH
F32, BF16 = jnp.float32, jnp.bfloat16
PLANES, CORES = 4, 2
GREETED_BY = ((1, 3), (2,), (0,), (2,))
ANSWERS = ((1, 3), (2,), (0,), (2,))
RUN = 4
TILE, LANES = 8, 128


def dot(a, b, dims):
    return lax.dot_general(
        a, b, ((dims[:1], dims[1:]), ((), ())), preferred_element_type=F32
    )


def halves(a):
    high = a.astype(BF16)
    return high, (a - high.astype(F32)).astype(BF16)


def dot3(a, b, dims):
    return dot(a[0], b[0], dims) + (dot(a[0], b[1], dims) + dot(a[1], b[0], dims))


def kernel(
    x_hbm, members_hbm, v_hbm, w_hbm, lam_hbm, c_hbm, e_hbm, near_hbm, coup_hbm, out_ref,
    x_ref, members_ref, v_ref, w_ref, lam_ref, c_ref, e_ref, near_ref, coup_ref,
    place_ref, cv_ref, ep_ref, base_ref,
    ends, ends_in, sel_out, sel_in, sum_out, sum_in, mix_out, mix_in,
    load_sem, answer_sem, ends_send, ends_recv, sel_send, sel_recv, sum_send, sum_recv,
    mix_send, mix_recv,
):
    sources, steps, panels = x_ref.shape
    clusters, size = members_ref.shape
    rank = c_ref.shape[1]
    rows = sources * steps
    times, spaces = lax.axis_size("tm"), lax.axis_size("space")
    near = spaces // PLANES
    tm, space = lax.axis_index("tm"), lax.axis_index("space")
    plane = space // CORES % PLANES
    spot = space // (PLANES * CORES) * CORES + space % CORES
    per_block = rank // near

    def peer(at_plane, at_spot):
        return at_spot // CORES * (PLANES * CORES) + at_plane * CORES + at_spot % CORES

    def each(low, high, act):
        if isinstance(low, int) and isinstance(high, int):
            for i in range(low, high):
                act(i)
            return

        def body(i, _):
            act(i)
            return _

        lax.fori_loop(low, high, body, 0)

    def each_time(act):
        runs = times // RUN
        low = tm // RUN < runs // 2
        for i in range(runs):
            run = jnp.where(low, runs - 1 - i, i)
            for turn in sorted(range(RUN), key=lambda n: -min(n, RUN - n)):
                other = run * RUN + (tm + turn) % RUN
                if turn or (runs > 1 and i < runs // 2):
                    act(other)
                else:
                    pl.when(other != tm)(lambda other=other: act(other))

    def spots(first):
        return sorted(range(first, near), key=lambda n: -min(n // CORES, (near - n) // CORES))

    def in_plane(which):
        return pl.when(plane == which)

    barrier = pltpu.get_barrier_semaphore()

    def greet(device):
        pl.semaphore_signal(barrier, inc=1, device_id=device, device_id_type=MESH)

    each_time(lambda other: greet((other, space)))
    for k in spots(1):
        greet((tm, peer(plane, (spot + k) % near)))
    for here in range(PLANES):

        @in_plane(here)
        def _():
            for to in range(PLANES):
                if here in GREETED_BY[to]:
                    for k in spots(0):
                        greet((tm, peer(to, (spot + k) % near)))

    loads = [
        pltpu.make_async_copy(src, dst, load_sem.at[i])
        for i, (src, dst) in enumerate(
            (
                (members_hbm, members_ref),
                (x_hbm, x_ref),
                (w_hbm, w_ref),
                (lam_hbm, lam_ref),
                (v_hbm, v_ref),
                (c_hbm, c_ref),
                (e_hbm, e_ref),
                (near_hbm, near_ref),
                (coup_hbm, coup_ref),
            )
        )
    ]
    for load in loads:
        load.start()

    loads[0].wait()
    panel_ids = lax.broadcasted_iota(jnp.int32, (panels, size), 0) + space * panels
    for c in range(clusters):
        place_ref[c] = jnp.where(panel_ids == members_ref[c : c + 1, :], 1.0, 0.0).astype(BF16)

    loads[1].wait()
    x = halves(x_ref[...].reshape(rows, panels))
    ordered = [[dot(half, place_ref[c], (1, 0)).astype(BF16) for half in x] for c in range(clusters)]
    loads[2].wait()
    loads[3].wait()

    lam = jnp.concatenate(
        [jnp.broadcast_to(lam_ref[c : c + 1, :], (sources, size)) for c in range(clusters)], axis=0
    )
    power = {1: 1.0 / (1.0 + lam)}
    n = 1
    while n < steps * times:
        power[2 * n] = power[n] * power[n]
        n *= 2

    local = []
    for c in range(clusters):
        modes = dot3(ordered[c], halves(w_ref[c]), (1, 1))
        own = slice(c * sources, c * sources + 1)
        z = (modes * power[1][own]).reshape(rows // TILE, TILE, size)
        row = lax.broadcasted_iota(jnp.int32, (TILE, size), 0)
        ramp = power[1][own]
        for n in (1, 2, 4):
            z = z + jnp.where(row >= n, power[n][own], 0.0)[None] * pltpu.roll(z, n, 1)
            ramp = ramp * jnp.where(row // n % 2 == 1, power[n][own], 1.0)
        z = z.reshape(sources, steps // TILE, TILE, size)
        blocks = [z[:, 0]]
        for b in range(1, steps // TILE):
            blocks.append(z[:, b] + ramp[None] * blocks[-1][:, TILE - 1 :, :])
        local.append((blocks, ramp))
        ends[c * sources : (c + 1) * sources, :] = blocks[-1][:, TILE - 1, :]

    far = jnp.where(plane == 0, len(GREETED_BY[0]) * near, near)
    pl.semaphore_wait(barrier, times - 1 + near - 1 + far)

    def copy(src, dst, send, recv, device):
        return pltpu.make_async_remote_copy(
            src_ref=src, dst_ref=dst, send_sem=send, recv_sem=recv,
            device_id=device, device_id_type=MESH,
        )

    each_time(
        lambda other: copy(
            ends, ends_in.at[(other - tm + times) % times - 1], ends_send, ends_recv, (other, space)
        ).start()
    )

    for here in range(PLANES):

        @in_plane(here)
        def _():
            for to in ANSWERS[here]:
                pl.semaphore_signal(
                    answer_sem, inc=1, device_id=(tm, peer(to, spot)), device_id_type=MESH
                )

    for load in loads[4:]:
        load.wait()
    coupled = [
        jnp.concatenate(
            [jnp.broadcast_to(ref[c : c + 1, :], (per_block, ref.shape[1])) for c in range(clusters)],
            axis=0,
        )
        for ref in (near_ref, coup_ref)
    ]
    spread = (TILE, spaces * TILE)
    lane = lax.broadcasted_iota(jnp.int32, spread, 1)
    select = jnp.zeros(spread, F32)
    for n in range(near_ref.shape[1]):
        hit = coupled[0][:, n : n + 1] == lane // per_block
        select = select + jnp.where(hit, coupled[1][:, n : n + 1], 0.0)
    same = lane % per_block == lax.broadcasted_iota(jnp.int32, spread, 0) % per_block
    sel_out[...] = jnp.where(same, select, 0.0)
    each(
        1, near,
        lambda k: copy(
            sel_out, sel_in.at[spot], sel_send, sel_recv, (tm, peer(plane, (spot + k) % near))
        ).start(),
    )
    sel_in[pl.ds(spot, 1)] = sel_out[...][None]

    cv_ref[...] = jnp.zeros_like(cv_ref)
    vectors = [halves(v_ref[c]) for c in range(clusters)]
    for c in range(clusters):
        at = slice(c * per_block, (c + 1) * per_block)
        cv = dot3(halves(c_ref[c]), vectors[c], (1, 0))
        spread_e = [dot(half, place_ref[c], (1, 1)) for half in halves(e_ref[c])]
        ep = spread_e[0] + spread_e[1]
        for b in range(near):
            block = slice(b * per_block, (b + 1) * per_block)
            cv_ref[b, at, c * size : (c + 1) * size] = cv[block]
            ep_ref[b, at, :] = ep[block]

    others = pl.ds(0, times - 1)
    pltpu.make_async_copy(ends_in.at[others], ends_in.at[others], ends_recv).wait()
    carry = ends[...]
    for k in range(times - 1, 0, -1):
        carry = carry * power[steps] + ends_in[k - 1]
    carry = carry / (1.0 - power[steps * times])

    solved = []
    for c in range(clusters):
        blocks, ramp = local[c]
        own = slice(c * sources, (c + 1) * sources)
        step = carry[own]
        parts = []
        for b in range(steps // TILE):
            parts.append(blocks[b] + ramp[None] * step[:, None, :])
            step = step * power[TILE][own]
        solved.append(halves(jnp.stack(parts, axis=1).reshape(rows, size)))
    compress = halves(cv_ref[...].reshape(rank * clusters, panels))
    summary = None
    for c in range(clusters):
        at = slice(c * size, (c + 1) * size)
        term = dot3([half[:, at] for half in compress], solved[c], (1, 1))
        summary = term if summary is None else summary + term
    summary = summary.reshape(near, TILE, rows)
    sum_out[...] = jnp.concatenate(
        [summary[:, :, i : i + LANES] for i in range(0, rows, LANES)], axis=1
    ).astype(BF16)

    def send_sum(to_plane, steps_on):
        for k in steps_on:
            to = (spot + k) % near
            copy(
                sum_out.at[to], sum_in.at[space], sum_send, sum_recv, (tm, peer(to_plane, to))
            ).start()

    for here in range(PLANES):

        @in_plane(here)
        def _():
            known = GREETED_BY[here]
            later = [to for to in range(PLANES) if to != here and to not in known]
            if here in (1, 3):
                known, later = (), [0, 2, 4 - here]
            for to in known:
                send_sum(to, spots(0))
            if known:
                send_sum(here, spots(1))
            pl.semaphore_wait(answer_sem, sum(here in answers for answers in ANSWERS))
            for to in later:
                send_sum(to, spots(0))
            if not known:
                send_sum(here, spots(1))

    sum_in[pl.ds(space, 1)] = sum_out[pl.ds(spot, 1)]

    base = None
    for c in range(clusters):
        for half in halves(dot3(solved[c], vectors[c], (1, 1))):
            term = dot(half, place_ref[c], (1, 1))
            base = term if base is None else base + term
    base_ref[...] = base
    expand = halves(-ep_ref[...].reshape(rank * clusters, panels))
    expand = jnp.concatenate([expand[0], expand[1], expand[0]], axis=0)

    plane_peers = pl.ds(0, near - 1)
    pltpu.make_async_copy(sel_in.at[plane_peers], sel_in.at[plane_peers], sel_recv).wait()
    selector = halves(sel_in[...].reshape(near * TILE, spaces * TILE))
    everyone = pl.ds(0, spaces - 1)
    pltpu.make_async_copy(sum_in.at[everyone], sum_in.at[everyone], sum_recv).wait()
    gathered = sum_in[...].astype(F32)
    for i in range(rows // LANES):
        part = gathered[:, i * TILE : (i + 1) * TILE, :].reshape(spaces * TILE, LANES).astype(BF16)
        mixed = dot(selector[0], part, (1, 0)) + dot(selector[1], part, (1, 0))
        mix_out[:, :, i * LANES : (i + 1) * LANES] = mixed.reshape(near, TILE, LANES)

    def send_mix(k):
        to = (spot + k) % near
        copy(mix_out.at[to], mix_in.at[spot], mix_send, mix_recv, (tm, peer(plane, to))).start()

    for k in spots(1):
        send_mix(k)
    mix_in[pl.ds(spot, 1)] = mix_out[pl.ds(spot, 1)]
    pltpu.make_async_copy(mix_in.at[plane_peers], mix_in.at[plane_peers], mix_recv).wait()

    mixed = halves(mix_in[...].reshape(rank * clusters, rows))
    mixed = jnp.concatenate([mixed[0], mixed[0], mixed[1]], axis=0)
    out_ref[...] = (base_ref[...] + dot(mixed, expand, (0, 0))).reshape(out_ref.shape)

    pltpu.make_async_copy(ends_in.at[others], ends_in.at[others], ends_send).wait()
    pltpu.make_async_copy(sel_in.at[plane_peers], sel_in.at[plane_peers], sel_send).wait()
    pltpu.make_async_copy(sum_in.at[everyone], sum_in.at[everyone], sum_send).wait()
    pltpu.make_async_copy(mix_in.at[plane_peers], mix_in.at[plane_peers], mix_send).wait()


def on_device(
    residual, members, eig_vectors, eig_left, eig_values, compress, expand, neighbors, coupling
):
    sources, steps, panels = residual.shape
    clusters, size = members.shape
    rank = compress.shape[1]
    rows = sources * steps
    times, spaces = lax.axis_size("tm"), lax.axis_size("space")
    near = spaces // PLANES
    assert clusters * sources == TILE and clusters * rank == near * TILE
    assert steps % TILE == 0 and rows == 2 * LANES and clusters * size == panels
    args = (
        residual, members, eig_vectors, eig_left, eig_values, compress,
        jnp.swapaxes(expand, 1, 2), neighbors, coupling,
    )
    carry = (clusters * sources, size)
    block = (2 * TILE, LANES)
    dma = pltpu.SemaphoreType.DMA
    return pl.pallas_call(
        kernel,
        out_shape=pltpu.VMEM(residual.shape, F32),
        in_specs=[pl.BlockSpec(memory_space=pltpu.HBM)] * len(args),
        out_specs=pl.BlockSpec(memory_space=pltpu.VMEM),
        scratch_shapes=[pltpu.VMEM(a.shape, a.dtype) for a in args]
        + [
            pltpu.VMEM((clusters, panels, size), BF16),
            pltpu.VMEM((near, TILE, panels), F32),
            pltpu.VMEM((near, TILE, panels), F32),
            pltpu.VMEM((rows, panels), F32),
            pltpu.VMEM(carry, F32),
            pltpu.VMEM((times - 1,) + carry, F32),
            pltpu.VMEM((TILE, spaces * TILE), F32),
            pltpu.VMEM((near, TILE, spaces * TILE), F32),
            pltpu.VMEM((near,) + block, BF16),
            pltpu.VMEM((spaces,) + block, BF16),
            pltpu.VMEM((near, TILE, rows), F32),
            pltpu.VMEM((near, TILE, rows), F32),
            dma((len(args),)),
            pltpu.SemaphoreType.REGULAR,
        ]
        + [dma(())] * 8,
        compiler_params=pltpu.CompilerParams(
            collective_id=0, has_side_effects=True, vmem_limit_bytes=32 * 1024 * 1024
        ),
    )(*(pltpu.with_memory_space_constraint(a, pltpu.HBM) for a in args))


def solution(mesh):
    return jax.shard_map(
        on_device,
        mesh=mesh,
        in_specs=(
            P(None, "tm", "space"),
            P("space", None),
            P("space", None, None),
            P("space", None, None),
            P("space", None),
            P("space", None, None),
            P("space", None, None),
            P("space", None),
            P("space", None),
        ),
        out_specs=P(None, "tm", "space"),
        check_vma=False,
    )
```

```python
import jax
import jax.numpy as jnp
from jax import lax
from jax.experimental import pallas as pl
from jax.experimental.pallas import tpu as pltpu
from jax.sharding import PartitionSpec as P

MESH = pl.DeviceIdType.MESH
F32, BF16 = jnp.float32, jnp.bfloat16
PLANES, CORES = 4, 2
EXACT = 4
RUN = 4
TILE, LANES = 8, 128


def dot(a, b, dims):
    return lax.dot_general(
        a, b, ((dims[:1], dims[1:]), ((), ())), preferred_element_type=F32
    )


def halves(a):
    high = a.astype(BF16)
    return high, (a - high.astype(F32)).astype(BF16)


def dot3(a, b, dims):
    return dot(a[0], b[0], dims) + (dot(a[0], b[1], dims) + dot(a[1], b[0], dims))


def kernel(
    x_hbm, members_hbm, v_hbm, w_hbm, lam_hbm, c_hbm, e_hbm, near_hbm, coup_hbm, out_ref,
    x_ref, members_ref, v_ref, w_ref, lam_ref, c_ref, e_ref, near_ref, coup_ref,
    place_ref, cv_ref, ep_ref, base_ref,
    ends, ends_in, short, short_in, sel_out, sel_in, sum_out, sum_in, mix_out, mix_in,
    load_sem, answer_sem, late_sem, ends_send, ends_recv, short_send, short_recv, sel_send, sel_recv, sum_send, sum_recv,
    mix_send, mix_recv,
):
    sources, steps, panels = x_ref.shape
    clusters, size = members_ref.shape
    rank = c_ref.shape[1]
    rows = sources * steps
    times, spaces = lax.axis_size("tm"), lax.axis_size("space")
    near = spaces // PLANES
    tm, space = lax.axis_index("tm"), lax.axis_index("space")
    plane = space // CORES % PLANES
    spot = space // (PLANES * CORES) * CORES + space % CORES
    per_block = rank // near

    def peer(at_plane, at_spot):
        return at_spot // CORES * (PLANES * CORES) + at_plane * CORES + at_spot % CORES

    def each(low, high, act):
        if isinstance(low, int) and isinstance(high, int):
            for i in range(low, high):
                act(i)
            return

        def body(i, _):
            act(i)
            return _

        lax.fori_loop(low, high, body, 0)

    def each_time(act):
        runs = times // RUN
        low = tm // RUN < runs // 2
        for i in range(runs):
            run = jnp.where(low, runs - 1 - i, i)
            for turn in sorted(range(RUN), key=lambda n: -min(n, RUN - n)):
                other = run * RUN + (tm + turn) % RUN
                if turn or (runs > 1 and i < runs // 2):
                    act(other)
                else:
                    pl.when(other != tm)(lambda other=other: act(other))

    def spots(first):
        return sorted(range(first, near), key=lambda n: min(n // CORES, (near - n) // CORES))

    def in_planes(*which):
        return pl.when(plane == which[0] if len(which) == 1 else plane % 2 == 1)

    barrier = pltpu.get_barrier_semaphore()

    def greet(device):
        pl.semaphore_signal(barrier, inc=1, device_id=device, device_id_type=MESH)

    @in_planes(2)
    def _():
        greet((tm, peer(1, spot)))
        greet((tm, peer(3, spot)))

    @in_planes(1, 3)
    def _():
        for k in spots(0):
            greet((tm, peer(0, (spot + k) % near)))

    each_time(lambda other: greet((other, space)))
    for k in spots(1):
        greet((tm, peer(plane, (spot + k) % near)))

    @in_planes(0)
    def _():
        for k in spots(0):
            greet((tm, peer(2, (spot + k) % near)))

    loads = [
        pltpu.make_async_copy(src, dst, load_sem.at[i])
        for i, (src, dst) in enumerate(
            (
                (members_hbm, members_ref),
                (x_hbm, x_ref),
                (w_hbm, w_ref),
                (lam_hbm, lam_ref),
                (v_hbm, v_ref),
                (c_hbm, c_ref),
                (e_hbm, e_ref),
                (near_hbm, near_ref),
                (coup_hbm, coup_ref),
            )
        )
    ]
    for load in loads:
        load.start()

    loads[0].wait()
    panel_ids = lax.broadcasted_iota(jnp.int32, (panels, size), 0) + space * panels
    for c in range(clusters):
        place_ref[c] = jnp.where(panel_ids == members_ref[c : c + 1, :], 1.0, 0.0).astype(BF16)

    loads[1].wait()
    x = halves(x_ref[...].reshape(rows, panels))
    ordered = [[dot(half, place_ref[c], (1, 0)).astype(BF16) for half in x] for c in range(clusters)]
    loads[2].wait()
    loads[3].wait()

    lam = jnp.concatenate(
        [jnp.broadcast_to(lam_ref[c : c + 1, :], (sources, size)) for c in range(clusters)], axis=0
    )
    power = {1: 1.0 / (1.0 + lam)}
    n = 1
    while n < steps * times:
        power[2 * n] = power[n] * power[n]
        n *= 2

    local = []
    for c in range(clusters):
        modes = dot3(ordered[c], halves(w_ref[c]), (1, 1))
        own = slice(c * sources, c * sources + 1)
        z = (modes * power[1][own]).reshape(rows // TILE, TILE, size)
        row = lax.broadcasted_iota(jnp.int32, (TILE, size), 0)
        ramp = power[1][own]
        for n in (1, 2, 4):
            z = z + jnp.where(row >= n, power[n][own], 0.0)[None] * pltpu.roll(z, n, 1)
            ramp = ramp * jnp.where(row // n % 2 == 1, power[n][own], 1.0)
        z = z.reshape(sources, steps // TILE, TILE, size)
        blocks = [z[:, 0]]
        for b in range(1, steps // TILE):
            blocks.append(z[:, b] + ramp[None] * blocks[-1][:, TILE - 1 :, :])
        local.append((blocks, ramp))
        ends[c * sources : (c + 1) * sources, :] = blocks[-1][:, TILE - 1, :]

    short[...] = jnp.concatenate(
        [ends[:, i : i + LANES] for i in range(0, size, LANES)], axis=0
    ).astype(BF16)

    far = jnp.where(plane == 0, 2 * near, jnp.where(plane == 2, near, 1))
    pl.semaphore_wait(barrier, times - 1 + near - 1 + far)

    def copy(src, dst, send, recv, device):
        return pltpu.make_async_remote_copy(
            src_ref=src, dst_ref=dst, send_sem=send, recv_sem=recv,
            device_id=device, device_id_type=MESH,
        )

    def answer(sem, to_plane):
        pl.semaphore_signal(
            sem, inc=1, device_id=(tm, peer(to_plane, spot)), device_id_type=MESH
        )

    @in_planes(0)
    def _():
        answer(answer_sem, 1)
        answer(answer_sem, 3)

    def send_ends(other):
        back = (other - tm + times) % times

        @pl.when(back > EXACT)
        def _():
            at = jnp.maximum(back - EXACT - 1, 0)
            copy(short, short_in.at[at], short_send, short_recv, (other, space)).start()

        @pl.when(back <= EXACT)
        def _():
            at = jnp.minimum(back - 1, EXACT - 1)
            copy(ends, ends_in.at[at], ends_send, ends_recv, (other, space)).start()

    each_time(send_ends)
    @in_planes(1, 3)
    def _():
        answer(answer_sem, 2)

    @in_planes(2)
    def _():
        answer(answer_sem, 0)

    for load in loads[4:]:
        load.wait()
    coupled = [
        jnp.concatenate(
            [jnp.broadcast_to(ref[c : c + 1, :], (per_block, ref.shape[1])) for c in range(clusters)],
            axis=0,
        )
        for ref in (near_ref, coup_ref)
    ]
    spread = (TILE, spaces * TILE)
    lane = lax.broadcasted_iota(jnp.int32, spread, 1)
    select = jnp.zeros(spread, F32)
    for n in range(near_ref.shape[1]):
        hit = coupled[0][:, n : n + 1] == lane // per_block
        select = select + jnp.where(hit, coupled[1][:, n : n + 1], 0.0)
    same = lane % per_block == lax.broadcasted_iota(jnp.int32, spread, 0) % per_block
    sel_out[...] = jnp.where(same, select, 0.0)
    each(
        1, near,
        lambda k: copy(
            sel_out, sel_in.at[spot], sel_send, sel_recv, (tm, peer(plane, (spot + k) % near))
        ).start(),
    )
    sel_in[pl.ds(spot, 1)] = sel_out[...][None]

    cv_ref[...] = jnp.zeros_like(cv_ref)
    vectors = [halves(v_ref[c]) for c in range(clusters)]
    for c in range(clusters):
        at = slice(c * per_block, (c + 1) * per_block)
        cv = dot3(halves(c_ref[c]), vectors[c], (1, 0))
        spread_e = [dot(half, place_ref[c], (1, 1)) for half in halves(e_ref[c])]
        ep = spread_e[0] + spread_e[1]
        for b in range(near):
            block = slice(b * per_block, (b + 1) * per_block)
            cv_ref[b, at, c * size : (c + 1) * size] = cv[block]
            ep_ref[b, at, :] = ep[block]

    pltpu.make_async_copy(short_in, short_in, short_recv).wait()
    pltpu.make_async_copy(ends_in, ends_in, ends_recv).wait()
    carry = ends[...]
    for k in range(times - 1, 0, -1):
        if k > EXACT:
            end = short_in[k - EXACT - 1].astype(F32)
            end = jnp.concatenate([end[i : i + TILE] for i in range(0, end.shape[0], TILE)], axis=1)
        else:
            end = ends_in[k - 1]
        carry = carry * power[steps] + end
    carry = carry / (1.0 - power[steps * times])

    solved = []
    for c in range(clusters):
        blocks, ramp = local[c]
        own = slice(c * sources, (c + 1) * sources)
        step = carry[own]
        parts = []
        for b in range(steps // TILE):
            parts.append(blocks[b] + ramp[None] * step[:, None, :])
            step = step * power[TILE][own]
        solved.append(halves(jnp.stack(parts, axis=1).reshape(rows, size)))
    compress = halves(cv_ref[...].reshape(rank * clusters, panels))
    summary = None
    for c in range(clusters):
        at = slice(c * size, (c + 1) * size)
        term = dot3([half[:, at] for half in compress], solved[c], (1, 1))
        summary = term if summary is None else summary + term
    summary = summary.reshape(near, TILE, rows)
    sum_out[...] = jnp.concatenate(
        [summary[:, :, i : i + LANES] for i in range(0, rows, LANES)], axis=1
    ).astype(BF16)

    def send_sum(to_plane, to_spots):
        for to in to_spots:
            copy(
                sum_out.at[to], sum_in.at[space], sum_send, sum_recv, (tm, peer(to_plane, to))
            ).start()

    def send_own():
        send_sum(plane, [(spot + k) % near for k in spots(1)])

    @in_planes(0)
    def _():
        send_own()
        send_sum(1, range(near))
        send_sum(3, range(near))
        pl.semaphore_wait(answer_sem, 1)
        send_sum(2, range(near))

    @in_planes(1, 3)
    def _():
        pl.semaphore_wait(answer_sem, 1)
        send_sum(0, range(near))
        send_own()
        send_sum(4 - plane, range(near))
        pl.semaphore_wait(late_sem, 1)
        send_sum(2, range(near))

    @in_planes(2)
    def _():
        send_sum(0, range(near))
        send_own()
        pl.semaphore_wait(answer_sem, 2)
        answer(late_sem, 1)
        answer(late_sem, 3)
        send_sum(1, range(near))
        send_sum(3, range(near))

    sum_in[pl.ds(space, 1)] = sum_out[pl.ds(spot, 1)]

    base = None
    for c in range(clusters):
        for half in halves(dot3(solved[c], vectors[c], (1, 1))):
            term = dot(half, place_ref[c], (1, 1))
            base = term if base is None else base + term
    base_ref[...] = base
    expand = halves(-ep_ref[...].reshape(rank * clusters, panels))
    expand = jnp.concatenate([expand[0], expand[1], expand[0]], axis=0)

    plane_peers = pl.ds(0, near - 1)
    pltpu.make_async_copy(sel_in.at[plane_peers], sel_in.at[plane_peers], sel_recv).wait()
    selector = halves(sel_in[...].reshape(near * TILE, spaces * TILE))
    everyone = pl.ds(0, spaces - 1)
    pltpu.make_async_copy(sum_in.at[everyone], sum_in.at[everyone], sum_recv).wait()
    gathered = sum_in[...].astype(F32)
    for i in range(rows // LANES):
        part = gathered[:, i * TILE : (i + 1) * TILE, :].reshape(spaces * TILE, LANES).astype(BF16)
        mixed = dot(selector[0], part, (1, 0)) + dot(selector[1], part, (1, 0))
        mix_out[:, :, i * LANES : (i + 1) * LANES] = mixed.reshape(near, TILE, LANES)

    def send_mix(k):
        to = (spot + k) % near
        copy(mix_out.at[to], mix_in.at[spot], mix_send, mix_recv, (tm, peer(plane, to))).start()

    for k in spots(1):
        send_mix(k)
    mix_in[pl.ds(spot, 1)] = mix_out[pl.ds(spot, 1)]
    pltpu.make_async_copy(mix_in.at[plane_peers], mix_in.at[plane_peers], mix_recv).wait()

    mixed = halves(mix_in[...].reshape(rank * clusters, rows))
    mixed = jnp.concatenate([mixed[0], mixed[0], mixed[1]], axis=0)
    out_ref[...] = (base_ref[...] + dot(mixed, expand, (0, 0))).reshape(out_ref.shape)

    pltpu.make_async_copy(short_in, short_in, short_send).wait()
    pltpu.make_async_copy(ends_in, ends_in, ends_send).wait()
    pltpu.make_async_copy(sel_in.at[plane_peers], sel_in.at[plane_peers], sel_send).wait()
    pltpu.make_async_copy(sum_in.at[everyone], sum_in.at[everyone], sum_send).wait()
    pltpu.make_async_copy(mix_in.at[plane_peers], mix_in.at[plane_peers], mix_send).wait()


def on_device(
    residual, members, eig_vectors, eig_left, eig_values, compress, expand, neighbors, coupling
):
    sources, steps, panels = residual.shape
    clusters, size = members.shape
    rank = compress.shape[1]
    rows = sources * steps
    times, spaces = lax.axis_size("tm"), lax.axis_size("space")
    near = spaces // PLANES
    assert clusters * sources == TILE and clusters * rank == near * TILE
    assert steps % TILE == 0 and rows == size == 2 * LANES and clusters * size == panels
    args = (
        residual, members, eig_vectors, eig_left, eig_values, compress,
        jnp.swapaxes(expand, 1, 2), neighbors, coupling,
    )
    carry = (clusters * sources, size)
    block = (2 * TILE, LANES)
    dma = pltpu.SemaphoreType.DMA
    return pl.pallas_call(
        kernel,
        out_shape=pltpu.VMEM(residual.shape, F32),
        in_specs=[pl.BlockSpec(memory_space=pltpu.HBM)] * len(args),
        out_specs=pl.BlockSpec(memory_space=pltpu.VMEM),
        scratch_shapes=[pltpu.VMEM(a.shape, a.dtype) for a in args]
        + [
            pltpu.VMEM((clusters, panels, size), BF16),
            pltpu.VMEM((near, TILE, panels), F32),
            pltpu.VMEM((near, TILE, panels), F32),
            pltpu.VMEM((rows, panels), F32),
            pltpu.VMEM(carry, F32),
            pltpu.VMEM((EXACT,) + carry, F32),
            pltpu.VMEM(block, BF16),
            pltpu.VMEM((times - 1 - EXACT,) + block, BF16),
            pltpu.VMEM((TILE, spaces * TILE), F32),
            pltpu.VMEM((near, TILE, spaces * TILE), F32),
            pltpu.VMEM((near,) + block, BF16),
            pltpu.VMEM((spaces,) + block, BF16),
            pltpu.VMEM((near, TILE, rows), F32),
            pltpu.VMEM((near, TILE, rows), F32),
            dma((len(args),)),
            pltpu.SemaphoreType.REGULAR,
            pltpu.SemaphoreType.REGULAR,
        ]
        + [dma(())] * 10,
        compiler_params=pltpu.CompilerParams(
            collective_id=0, has_side_effects=True, vmem_limit_bytes=32 * 1024 * 1024
        ),
    )(*(pltpu.with_memory_space_constraint(a, pltpu.HBM) for a in args))


def solution(mesh):
    return jax.shard_map(
        on_device,
        mesh=mesh,
        in_specs=(
            P(None, "tm", "space"),
            P("space", None),
            P("space", None, None),
            P("space", None, None),
            P("space", None),
            P("space", None, None),
            P("space", None, None),
            P("space", None),
            P("space", None),
        ),
        out_specs=P(None, "tm", "space"),
        check_vma=False,
    )
```

```python
import jax
import jax.numpy as jnp
from jax import lax
from jax.experimental import pallas as pl
from jax.experimental.pallas import tpu as pltpu
from jax.sharding import PartitionSpec as P

MESH = pl.DeviceIdType.MESH
F32, BF16 = jnp.float32, jnp.bfloat16
PLANES, CORES = 4, 2
EXACT = 4
RUN = 4
TILE, LANES = 8, 128


def dot(a, b, dims):
    return lax.dot_general(
        a, b, ((dims[:1], dims[1:]), ((), ())), preferred_element_type=F32
    )


def halves(a):
    high = a.astype(BF16)
    return high, (a - high.astype(F32)).astype(BF16)


def dot3(a, b, dims):
    return dot(a[0], b[0], dims) + (dot(a[0], b[1], dims) + dot(a[1], b[0], dims))


def kernel(
    x_hbm, members_hbm, v_hbm, w_hbm, lam_hbm, c_hbm, e_hbm, near_hbm, coup_hbm, out_ref,
    x_ref, members_ref, v_ref, w_ref, lam_ref, c_ref, e_ref, near_ref, coup_ref,
    place_ref, cv_ref, ep_ref, base_ref,
    ends, ends_in, short, short_in, sel_out, sel_in, sum_out, sum_in, mix_out, mix_in,
    load_sem, answer_sem, late_sem, ends_send, ends_recv, short_send, short_recv, sel_send, sel_recv, sum_send, sum_recv,
    mix_send, mix_recv,
):
    sources, steps, panels = x_ref.shape
    clusters, size = members_ref.shape
    rank = c_ref.shape[1]
    rows = sources * steps
    times, spaces = lax.axis_size("tm"), lax.axis_size("space")
    near = spaces // PLANES
    tm, space = lax.axis_index("tm"), lax.axis_index("space")
    plane = space // CORES % PLANES
    spot = space // (PLANES * CORES) * CORES + space % CORES
    per_block = rank // near

    def peer(at_plane, at_spot):
        return at_spot // CORES * (PLANES * CORES) + at_plane * CORES + at_spot % CORES

    def each(low, high, act):
        if isinstance(low, int) and isinstance(high, int):
            for i in range(low, high):
                act(i)
            return

        def body(i, _):
            act(i)
            return _

        lax.fori_loop(low, high, body, 0)

    def each_time(act):
        runs = times // RUN
        low = tm // RUN < runs // 2
        for i in range(runs):
            run = jnp.where(low, runs - 1 - i, i)
            for turn in sorted(range(RUN), key=lambda n: -min(n, RUN - n)):
                other = run * RUN + (tm + turn) % RUN
                if turn or (runs > 1 and i < runs // 2):
                    act(other)
                else:
                    pl.when(other != tm)(lambda other=other: act(other))

    def spots(first):
        return sorted(range(first, near), key=lambda n: min(n // CORES, (near - n) // CORES))

    far_first = sorted(range(near), key=lambda n: -min(n, near - n))

    def in_planes(*which):
        return pl.when(plane == which[0] if len(which) == 1 else plane % 2 == 1)

    barrier = pltpu.get_barrier_semaphore()

    def greet(device):
        pl.semaphore_signal(barrier, inc=1, device_id=device, device_id_type=MESH)

    @in_planes(2)
    def _():
        greet((tm, peer(1, spot)))
        greet((tm, peer(3, spot)))

    @in_planes(1, 3)
    def _():
        for k in spots(0):
            greet((tm, peer(0, (spot + k) % near)))

    @in_planes(0)
    def _():
        for k in spots(0):
            greet((tm, peer(2, (spot + k) % near)))

    each_time(lambda other: greet((other, space)))
    for k in spots(1):
        greet((tm, peer(plane, (spot + k) % near)))

    loads = [
        pltpu.make_async_copy(src, dst, load_sem.at[i])
        for i, (src, dst) in enumerate(
            (
                (members_hbm, members_ref),
                (x_hbm, x_ref),
                (w_hbm, w_ref),
                (lam_hbm, lam_ref),
                (v_hbm, v_ref),
                (c_hbm, c_ref),
                (e_hbm, e_ref),
                (near_hbm, near_ref),
                (coup_hbm, coup_ref),
            )
        )
    ]
    for load in loads:
        load.start()

    loads[0].wait()
    panel_ids = lax.broadcasted_iota(jnp.int32, (panels, size), 0) + space * panels
    for c in range(clusters):
        place_ref[c] = jnp.where(panel_ids == members_ref[c : c + 1, :], 1.0, 0.0).astype(BF16)

    loads[1].wait()
    x = halves(x_ref[...].reshape(rows, panels))
    ordered = [[dot(half, place_ref[c], (1, 0)).astype(BF16) for half in x] for c in range(clusters)]
    loads[2].wait()
    loads[3].wait()

    lam = jnp.concatenate(
        [jnp.broadcast_to(lam_ref[c : c + 1, :], (sources, size)) for c in range(clusters)], axis=0
    )
    power = {1: 1.0 / (1.0 + lam)}
    n = 1
    while n < steps * times:
        power[2 * n] = power[n] * power[n]
        n *= 2

    local = []
    for c in range(clusters):
        modes = dot3(ordered[c], halves(w_ref[c]), (1, 1))
        own = slice(c * sources, c * sources + 1)
        z = (modes * power[1][own]).reshape(rows // TILE, TILE, size)
        row = lax.broadcasted_iota(jnp.int32, (TILE, size), 0)
        ramp = power[1][own]
        for n in (1, 2, 4):
            z = z + jnp.where(row >= n, power[n][own], 0.0)[None] * pltpu.roll(z, n, 1)
            ramp = ramp * jnp.where(row // n % 2 == 1, power[n][own], 1.0)
        z = z.reshape(sources, steps // TILE, TILE, size)
        blocks = [z[:, 0]]
        for b in range(1, steps // TILE):
            blocks.append(z[:, b] + ramp[None] * blocks[-1][:, TILE - 1 :, :])
        local.append((blocks, ramp))
        ends[c * sources : (c + 1) * sources, :] = blocks[-1][:, TILE - 1, :]

    short[...] = jnp.concatenate(
        [ends[:, i : i + LANES] for i in range(0, size, LANES)], axis=0
    ).astype(BF16)

    far = jnp.where(plane == 0, 2 * near, jnp.where(plane == 2, near, 1))
    pl.semaphore_wait(barrier, times - 1 + near - 1 + far)

    def copy(src, dst, send, recv, device):
        return pltpu.make_async_remote_copy(
            src_ref=src, dst_ref=dst, send_sem=send, recv_sem=recv,
            device_id=device, device_id_type=MESH,
        )

    def answer(sem, to_plane):
        pl.semaphore_signal(
            sem, inc=1, device_id=(tm, peer(to_plane, spot)), device_id_type=MESH
        )

    @in_planes(0)
    def _():
        answer(answer_sem, 1)
        answer(answer_sem, 3)

    def send_ends(other):
        back = (other - tm + times) % times

        @pl.when(back > EXACT)
        def _():
            at = jnp.maximum(back - EXACT - 1, 0)
            copy(short, short_in.at[at], short_send, short_recv, (other, space)).start()

        @pl.when(back <= EXACT)
        def _():
            at = jnp.minimum(back - 1, EXACT - 1)
            copy(ends, ends_in.at[at], ends_send, ends_recv, (other, space)).start()

    each_time(send_ends)
    @in_planes(1, 3)
    def _():
        answer(answer_sem, 2)

    @in_planes(2)
    def _():
        answer(answer_sem, 0)

    for load in loads[4:]:
        load.wait()
    coupled = [
        jnp.concatenate(
            [jnp.broadcast_to(ref[c : c + 1, :], (per_block, ref.shape[1])) for c in range(clusters)],
            axis=0,
        )
        for ref in (near_ref, coup_ref)
    ]
    spread = (TILE, spaces * TILE)
    lane = lax.broadcasted_iota(jnp.int32, spread, 1)
    select = jnp.zeros(spread, F32)
    for n in range(near_ref.shape[1]):
        hit = coupled[0][:, n : n + 1] == lane // per_block
        select = select + jnp.where(hit, coupled[1][:, n : n + 1], 0.0)
    same = lane % per_block == lax.broadcasted_iota(jnp.int32, spread, 0) % per_block
    sel_out[...] = jnp.where(same, select, 0.0)
    each(
        1, near,
        lambda k: copy(
            sel_out, sel_in.at[spot], sel_send, sel_recv, (tm, peer(plane, (spot + k) % near))
        ).start(),
    )
    sel_in[pl.ds(spot, 1)] = sel_out[...][None]

    cv_ref[...] = jnp.zeros_like(cv_ref)
    vectors = [halves(v_ref[c]) for c in range(clusters)]
    for c in range(clusters):
        at = slice(c * per_block, (c + 1) * per_block)
        cv = dot3(halves(c_ref[c]), vectors[c], (1, 0))
        spread_e = [dot(half, place_ref[c], (1, 1)) for half in halves(e_ref[c])]
        ep = spread_e[0] + spread_e[1]
        for b in range(near):
            block = slice(b * per_block, (b + 1) * per_block)
            cv_ref[b, at, c * size : (c + 1) * size] = cv[block]
            ep_ref[b, at, :] = ep[block]

    pltpu.make_async_copy(short_in, short_in, short_recv).wait()
    pltpu.make_async_copy(ends_in, ends_in, ends_recv).wait()
    carry = ends[...]
    for k in range(times - 1, 0, -1):
        if k > EXACT:
            end = short_in[k - EXACT - 1].astype(F32)
            end = jnp.concatenate([end[i : i + TILE] for i in range(0, end.shape[0], TILE)], axis=1)
        else:
            end = ends_in[k - 1]
        carry = carry * power[steps] + end
    carry = carry / (1.0 - power[steps * times])

    solved = []
    for c in range(clusters):
        blocks, ramp = local[c]
        own = slice(c * sources, (c + 1) * sources)
        step = carry[own]
        parts = []
        for b in range(steps // TILE):
            parts.append(blocks[b] + ramp[None] * step[:, None, :])
            step = step * power[TILE][own]
        solved.append(halves(jnp.stack(parts, axis=1).reshape(rows, size)))
    compress = halves(cv_ref[...].reshape(rank * clusters, panels))
    summary = None
    for c in range(clusters):
        at = slice(c * size, (c + 1) * size)
        term = dot3([half[:, at] for half in compress], solved[c], (1, 1))
        summary = term if summary is None else summary + term
    summary = summary.reshape(near, TILE, rows)
    sum_out[...] = jnp.concatenate(
        [summary[:, :, i : i + LANES] for i in range(0, rows, LANES)], axis=1
    ).astype(BF16)

    def send_sum(to_plane, to_spots):
        for to in to_spots:
            copy(
                sum_out.at[to], sum_in.at[space], sum_send, sum_recv, (tm, peer(to_plane, to))
            ).start()

    def send_own():
        send_sum(plane, [(spot + k) % near for k in spots(1)])

    @in_planes(0)
    def _():
        send_own()
        send_sum(1, range(near))
        send_sum(3, range(near))
        pl.semaphore_wait(answer_sem, 1)
        send_sum(2, range(near))

    @in_planes(1, 3)
    def _():
        pl.semaphore_wait(answer_sem, 1)
        send_sum(0, range(near))
        send_own()
        send_sum(4 - plane, range(near))
        pl.semaphore_wait(late_sem, 1)
        send_sum(2, range(near))

    @in_planes(2)
    def _():
        send_sum(0, [(spot + k) % near for k in far_first])
        send_own()
        pl.semaphore_wait(answer_sem, 2)
        answer(late_sem, 1)
        answer(late_sem, 3)
        send_sum(1, range(near))
        send_sum(3, range(near))

    sum_in[pl.ds(space, 1)] = sum_out[pl.ds(spot, 1)]

    base = None
    for c in range(clusters):
        for half in halves(dot3(solved[c], vectors[c], (1, 1))):
            term = dot(half, place_ref[c], (1, 1))
            base = term if base is None else base + term
    base_ref[...] = base
    expand = halves(-ep_ref[...].reshape(rank * clusters, panels))
    expand = jnp.concatenate([expand[0], expand[1], expand[0]], axis=0)

    plane_peers = pl.ds(0, near - 1)
    pltpu.make_async_copy(sel_in.at[plane_peers], sel_in.at[plane_peers], sel_recv).wait()
    selector = halves(sel_in[...].reshape(near * TILE, spaces * TILE))
    everyone = pl.ds(0, spaces - 1)
    pltpu.make_async_copy(sum_in.at[everyone], sum_in.at[everyone], sum_recv).wait()
    gathered = sum_in[...].astype(F32)
    for i in range(rows // LANES):
        part = gathered[:, i * TILE : (i + 1) * TILE, :].reshape(spaces * TILE, LANES).astype(BF16)
        mixed = dot(selector[0], part, (1, 0)) + dot(selector[1], part, (1, 0))
        mix_out[:, :, i * LANES : (i + 1) * LANES] = mixed.reshape(near, TILE, LANES)

    def send_mix(to):
        copy(mix_out.at[to], mix_in.at[spot], mix_send, mix_recv, (tm, peer(plane, to))).start()

    for k in far_first:
        if k:
            send_mix((spot + k) % near)
    mix_in[pl.ds(spot, 1)] = mix_out[pl.ds(spot, 1)]
    pltpu.make_async_copy(mix_in.at[plane_peers], mix_in.at[plane_peers], mix_recv).wait()

    mixed = halves(mix_in[...].reshape(rank * clusters, rows))
    mixed = jnp.concatenate([mixed[0], mixed[0], mixed[1]], axis=0)
    out_ref[...] = (base_ref[...] + dot(mixed, expand, (0, 0))).reshape(out_ref.shape)

    pltpu.make_async_copy(short_in, short_in, short_send).wait()
    pltpu.make_async_copy(ends_in, ends_in, ends_send).wait()
    pltpu.make_async_copy(sel_in.at[plane_peers], sel_in.at[plane_peers], sel_send).wait()
    pltpu.make_async_copy(sum_in.at[everyone], sum_in.at[everyone], sum_send).wait()
    pltpu.make_async_copy(mix_in.at[plane_peers], mix_in.at[plane_peers], mix_send).wait()


def on_device(
    residual, members, eig_vectors, eig_left, eig_values, compress, expand, neighbors, coupling
):
    sources, steps, panels = residual.shape
    clusters, size = members.shape
    rank = compress.shape[1]
    rows = sources * steps
    times, spaces = lax.axis_size("tm"), lax.axis_size("space")
    near = spaces // PLANES
    assert clusters * sources == TILE and clusters * rank == near * TILE
    assert steps % TILE == 0 and rows == size == 2 * LANES and clusters * size == panels
    args = (
        residual, members, eig_vectors, eig_left, eig_values, compress,
        jnp.swapaxes(expand, 1, 2), neighbors, coupling,
    )
    carry = (clusters * sources, size)
    block = (2 * TILE, LANES)
    dma = pltpu.SemaphoreType.DMA
    return pl.pallas_call(
        kernel,
        out_shape=pltpu.VMEM(residual.shape, F32),
        in_specs=[pl.BlockSpec(memory_space=pltpu.HBM)] * len(args),
        out_specs=pl.BlockSpec(memory_space=pltpu.VMEM),
        scratch_shapes=[pltpu.VMEM(a.shape, a.dtype) for a in args]
        + [
            pltpu.VMEM((clusters, panels, size), BF16),
            pltpu.VMEM((near, TILE, panels), F32),
            pltpu.VMEM((near, TILE, panels), F32),
            pltpu.VMEM((rows, panels), F32),
            pltpu.VMEM(carry, F32),
            pltpu.VMEM((EXACT,) + carry, F32),
            pltpu.VMEM(block, BF16),
            pltpu.VMEM((times - 1 - EXACT,) + block, BF16),
            pltpu.VMEM((TILE, spaces * TILE), F32),
            pltpu.VMEM((near, TILE, spaces * TILE), F32),
            pltpu.VMEM((near,) + block, BF16),
            pltpu.VMEM((spaces,) + block, BF16),
            pltpu.VMEM((near, TILE, rows), F32),
            pltpu.VMEM((near, TILE, rows), F32),
            dma((len(args),)),
            pltpu.SemaphoreType.REGULAR,
            pltpu.SemaphoreType.REGULAR,
        ]
        + [dma(())] * 10,
        compiler_params=pltpu.CompilerParams(
            collective_id=0, has_side_effects=True, vmem_limit_bytes=32 * 1024 * 1024
        ),
    )(*(pltpu.with_memory_space_constraint(a, pltpu.HBM) for a in args))


def solution(mesh):
    return jax.shard_map(
        on_device,
        mesh=mesh,
        in_specs=(
            P(None, "tm", "space"),
            P("space", None),
            P("space", None, None),
            P("space", None, None),
            P("space", None),
            P("space", None, None),
            P("space", None, None),
            P("space", None),
            P("space", None),
        ),
        out_specs=P(None, "tm", "space"),
        check_vma=False,
    )
```

```python
import jax
import jax.numpy as jnp
from jax import lax
from jax.experimental import pallas as pl
from jax.experimental.pallas import tpu as pltpu
from jax.sharding import PartitionSpec as P

MESH = pl.DeviceIdType.MESH
F32, BF16 = jnp.float32, jnp.bfloat16
PLANES, CORES = 4, 2
EXACT = 4
RUN = 4
TILE, LANES = 8, 128


def dot(a, b, dims):
    return lax.dot_general(
        a, b, ((dims[:1], dims[1:]), ((), ())), preferred_element_type=F32
    )


def halves(a):
    high = a.astype(BF16)
    return high, (a - high.astype(F32)).astype(BF16)


def dot3(a, b, dims):
    return dot(a[0], b[0], dims) + (dot(a[0], b[1], dims) + dot(a[1], b[0], dims))


def kernel(
    x_hbm, members_hbm, v_hbm, w_hbm, lam_hbm, c_hbm, e_hbm, near_hbm, coup_hbm, out_ref,
    x_ref, members_ref, v_ref, w_ref, lam_ref, c_ref, e_ref, near_ref, coup_ref,
    place_ref, cv_ref, ep_ref, base_ref,
    ends, ends_in, short, short_in, sel_out, sel_in, sum_out, sum_in, mix_out, mix_in,
    load_sem, answer_sem, late_sem, ends_send, ends_recv, short_send, short_recv, sel_send, sel_recv, sum_send, sum_recv,
    mix_send, mix_recv,
):
    sources, steps, panels = x_ref.shape
    clusters, size = members_ref.shape
    rank = c_ref.shape[1]
    rows = sources * steps
    times, spaces = lax.axis_size("tm"), lax.axis_size("space")
    near = spaces // PLANES
    tm, space = lax.axis_index("tm"), lax.axis_index("space")
    plane = space // CORES % PLANES
    spot = space // (PLANES * CORES) * CORES + space % CORES
    per_block = rank // near

    def peer(at_plane, at_spot):
        return at_spot // CORES * (PLANES * CORES) + at_plane * CORES + at_spot % CORES

    def each(low, high, act):
        if isinstance(low, int) and isinstance(high, int):
            for i in range(low, high):
                act(i)
            return

        def body(i, _):
            act(i)
            return _

        lax.fori_loop(low, high, body, 0)

    def each_time(act):
        runs = times // RUN
        low = tm // RUN < runs // 2
        for i in range(runs):
            run = jnp.where(low, runs - 1 - i, i)
            for turn in sorted(range(RUN), key=lambda n: -min(n, RUN - n)):
                other = run * RUN + (tm + turn) % RUN
                if turn or (runs > 1 and i < runs // 2):
                    act(other)
                else:
                    pl.when(other != tm)(lambda other=other: act(other))

    def spots(first):
        return sorted(range(first, near), key=lambda n: min(n // CORES, (near - n) // CORES))

    far_first = sorted(range(near), key=lambda n: -min(n, near - n))

    def in_planes(*which):
        return pl.when(plane == which[0] if len(which) == 1 else plane % 2 == 1)

    barrier = pltpu.get_barrier_semaphore()

    def greet(device):
        pl.semaphore_signal(barrier, inc=1, device_id=device, device_id_type=MESH)

    @in_planes(2)
    def _():
        greet((tm, peer(1, spot)))
        greet((tm, peer(3, spot)))

    @in_planes(1, 3)
    def _():
        for k in spots(0):
            greet((tm, peer(0, (spot + k) % near)))

    @in_planes(0)
    def _():
        for k in spots(0):
            greet((tm, peer(2, (spot + k) % near)))

    each_time(lambda other: greet((other, space)))
    for k in spots(1):
        greet((tm, peer(plane, (spot + k) % near)))

    loads = [
        pltpu.make_async_copy(src, dst, load_sem.at[i])
        for i, (src, dst) in enumerate(
            (
                (members_hbm, members_ref),
                (x_hbm, x_ref),
                (w_hbm, w_ref),
                (lam_hbm, lam_ref),
                (v_hbm, v_ref),
                (c_hbm, c_ref),
                (e_hbm, e_ref),
                (near_hbm, near_ref),
                (coup_hbm, coup_ref),
            )
        )
    ]
    for load in loads:
        load.start()

    loads[0].wait()
    panel_ids = lax.broadcasted_iota(jnp.int32, (panels, size), 0) + space * panels
    for c in range(clusters):
        place_ref[c] = jnp.where(panel_ids == members_ref[c : c + 1, :], 1.0, 0.0).astype(BF16)

    loads[1].wait()
    x = halves(x_ref[...].reshape(rows, panels))
    ordered = [[dot(half, place_ref[c], (1, 0)).astype(BF16) for half in x] for c in range(clusters)]
    loads[2].wait()
    loads[3].wait()

    lam = jnp.concatenate(
        [jnp.broadcast_to(lam_ref[c : c + 1, :], (sources, size)) for c in range(clusters)], axis=0
    )
    power = {1: 1.0 / (1.0 + lam)}
    n = 1
    while n < steps * times:
        power[2 * n] = power[n] * power[n]
        n *= 2

    local = []
    for c in range(clusters):
        modes = dot3(ordered[c], halves(w_ref[c]), (1, 1))
        own = slice(c * sources, c * sources + 1)
        z = (modes * power[1][own]).reshape(rows // TILE, TILE, size)
        row = lax.broadcasted_iota(jnp.int32, (TILE, size), 0)
        ramp = power[1][own]
        for n in (1, 2, 4):
            z = z + jnp.where(row >= n, power[n][own], 0.0)[None] * pltpu.roll(z, n, 1)
            ramp = ramp * jnp.where(row // n % 2 == 1, power[n][own], 1.0)
        z = z.reshape(sources, steps // TILE, TILE, size)
        blocks = [z[:, 0]]
        for b in range(1, steps // TILE):
            blocks.append(z[:, b] + ramp[None] * blocks[-1][:, TILE - 1 :, :])
        local.append((blocks, ramp))
        ends[c * sources : (c + 1) * sources, :] = blocks[-1][:, TILE - 1, :]

    short[...] = jnp.concatenate(
        [ends[:, i : i + LANES] for i in range(0, size, LANES)], axis=0
    ).astype(BF16)

    far = jnp.where(plane == 0, 2 * near, jnp.where(plane == 2, near, 1))
    pl.semaphore_wait(barrier, times - 1 + near - 1 + far)

    def copy(src, dst, send, recv, device):
        return pltpu.make_async_remote_copy(
            src_ref=src, dst_ref=dst, send_sem=send, recv_sem=recv,
            device_id=device, device_id_type=MESH,
        )

    def answer(sem, to_plane):
        pl.semaphore_signal(
            sem, inc=1, device_id=(tm, peer(to_plane, spot)), device_id_type=MESH
        )

    @in_planes(0)
    def _():
        answer(answer_sem, 1)
        answer(answer_sem, 3)

    def send_ends(other):
        back = (other - tm + times) % times

        @pl.when(back > EXACT)
        def _():
            at = jnp.maximum(back - EXACT - 1, 0)
            copy(short, short_in.at[at], short_send, short_recv, (other, space)).start()

        @pl.when(back <= EXACT)
        def _():
            at = jnp.minimum(back - 1, EXACT - 1)
            copy(ends, ends_in.at[at], ends_send, ends_recv, (other, space)).start()

    each_time(send_ends)
    @in_planes(1, 3)
    def _():
        answer(answer_sem, 2)

    @in_planes(2)
    def _():
        answer(answer_sem, 0)

    for load in loads[4:]:
        load.wait()
    coupled = [
        jnp.concatenate(
            [jnp.broadcast_to(ref[c : c + 1, :], (per_block, ref.shape[1])) for c in range(clusters)],
            axis=0,
        )
        for ref in (near_ref, coup_ref)
    ]
    spread = (TILE, spaces * TILE)
    lane = lax.broadcasted_iota(jnp.int32, spread, 1)
    select = jnp.zeros(spread, F32)
    for n in range(near_ref.shape[1]):
        hit = coupled[0][:, n : n + 1] == lane // per_block
        select = select + jnp.where(hit, coupled[1][:, n : n + 1], 0.0)
    same = lane % per_block == lax.broadcasted_iota(jnp.int32, spread, 0) % per_block
    sel_out[...] = jnp.where(same, select, 0.0)
    sel_in[pl.ds(spot, 1)] = sel_out[...][None]

    cv_ref[...] = jnp.zeros_like(cv_ref)
    vectors = [halves(v_ref[c]) for c in range(clusters)]
    for c in range(clusters):
        at = slice(c * per_block, (c + 1) * per_block)
        cv = dot3(halves(c_ref[c]), vectors[c], (1, 0))
        spread_e = [dot(half, place_ref[c], (1, 1)) for half in halves(e_ref[c])]
        ep = spread_e[0] + spread_e[1]
        for b in range(near):
            block = slice(b * per_block, (b + 1) * per_block)
            cv_ref[b, at, c * size : (c + 1) * size] = cv[block]
            ep_ref[b, at, :] = ep[block]

    compress = halves(cv_ref[...].reshape(rank * clusters, panels))
    round_period = 1.0 / (1.0 - power[steps * times])
    pltpu.make_async_copy(short_in, short_in, short_recv).wait()
    pltpu.make_async_copy(ends_in, ends_in, ends_recv).wait()
    carry = ends[...]
    for k in range(times - 1, 0, -1):
        if k > EXACT:
            end = short_in[k - EXACT - 1].astype(F32)
            end = jnp.concatenate([end[i : i + TILE] for i in range(0, end.shape[0], TILE)], axis=1)
        else:
            end = ends_in[k - 1]
        carry = carry * power[steps] + end
    carry = carry * round_period

    solved = []
    for c in range(clusters):
        blocks, ramp = local[c]
        own = slice(c * sources, (c + 1) * sources)
        step = carry[own]
        parts = []
        for b in range(steps // TILE):
            parts.append(blocks[b] + ramp[None] * step[:, None, :])
            step = step * power[TILE][own]
        solved.append(halves(jnp.stack(parts, axis=1).reshape(rows, size)))
    summary = None
    for c in range(clusters):
        at = slice(c * size, (c + 1) * size)
        term = dot3([half[:, at] for half in compress], solved[c], (1, 1))
        summary = term if summary is None else summary + term
    summary = summary.reshape(near, TILE, rows)
    sum_out[...] = jnp.concatenate(
        [summary[:, :, i : i + LANES] for i in range(0, rows, LANES)], axis=1
    ).astype(BF16)

    def send_sum(to_plane, to_spots):
        for to in to_spots:
            copy(
                sum_out.at[to], sum_in.at[space], sum_send, sum_recv, (tm, peer(to_plane, to))
            ).start()

    def send_own():
        send_sum(plane, [(spot + k) % near for k in spots(1)])

    @in_planes(0)
    def _():
        send_own()
        send_sum(1, range(near))
        send_sum(3, range(near))
        pl.semaphore_wait(answer_sem, 1)
        send_sum(2, range(near))

    @in_planes(1, 3)
    def _():
        pl.semaphore_wait(answer_sem, 1)
        send_sum(0, range(near))
        send_own()
        send_sum(4 - plane, range(near))
        pl.semaphore_wait(late_sem, 1)
        send_sum(2, range(near))

    @in_planes(2)
    def _():
        send_sum(0, [(spot + k) % near for k in far_first])
        send_own()
        pl.semaphore_wait(answer_sem, 2)
        answer(late_sem, 1)
        answer(late_sem, 3)
        send_sum(1, range(near))
        send_sum(3, range(near))

    sum_in[pl.ds(space, 1)] = sum_out[pl.ds(spot, 1)]

    each(
        1, near,
        lambda k: copy(
            sel_out, sel_in.at[spot], sel_send, sel_recv, (tm, peer(plane, (spot + k) % near))
        ).start(),
    )
    base = None
    for c in range(clusters):
        for half in halves(dot3(solved[c], vectors[c], (1, 1))):
            term = dot(half, place_ref[c], (1, 1))
            base = term if base is None else base + term
    base_ref[...] = base
    expand = halves(-ep_ref[...].reshape(rank * clusters, panels))
    expand = jnp.concatenate([expand[0], expand[1], expand[0]], axis=0)

    plane_peers = pl.ds(0, near - 1)
    pltpu.make_async_copy(sel_in.at[plane_peers], sel_in.at[plane_peers], sel_recv).wait()
    selector = halves(sel_in[...].reshape(near * TILE, spaces * TILE))
    everyone = pl.ds(0, spaces - 1)
    pltpu.make_async_copy(sum_in.at[everyone], sum_in.at[everyone], sum_recv).wait()
    gathered = sum_in[...].astype(F32)
    for i in range(rows // LANES):
        part = gathered[:, i * TILE : (i + 1) * TILE, :].reshape(spaces * TILE, LANES).astype(BF16)
        mixed = dot(selector[0], part, (1, 0)) + dot(selector[1], part, (1, 0))
        mix_out[:, :, i * LANES : (i + 1) * LANES] = mixed.reshape(near, TILE, LANES)

    def send_mix(to):
        copy(mix_out.at[to], mix_in.at[spot], mix_send, mix_recv, (tm, peer(plane, to))).start()

    for k in far_first:
        if k:
            send_mix((spot + k) % near)
    mix_in[pl.ds(spot, 1)] = mix_out[pl.ds(spot, 1)]
    pltpu.make_async_copy(mix_in.at[plane_peers], mix_in.at[plane_peers], mix_recv).wait()

    mixed = halves(mix_in[...].reshape(rank * clusters, rows))
    mixed = jnp.concatenate([mixed[0], mixed[0], mixed[1]], axis=0)
    out_ref[...] = (base_ref[...] + dot(mixed, expand, (0, 0))).reshape(out_ref.shape)

    pltpu.make_async_copy(short_in, short_in, short_send).wait()
    pltpu.make_async_copy(ends_in, ends_in, ends_send).wait()
    pltpu.make_async_copy(sel_in.at[plane_peers], sel_in.at[plane_peers], sel_send).wait()
    pltpu.make_async_copy(sum_in.at[everyone], sum_in.at[everyone], sum_send).wait()
    pltpu.make_async_copy(mix_in.at[plane_peers], mix_in.at[plane_peers], mix_send).wait()


def on_device(
    residual, members, eig_vectors, eig_left, eig_values, compress, expand, neighbors, coupling
):
    sources, steps, panels = residual.shape
    clusters, size = members.shape
    rank = compress.shape[1]
    rows = sources * steps
    times, spaces = lax.axis_size("tm"), lax.axis_size("space")
    near = spaces // PLANES
    assert clusters * sources == TILE and clusters * rank == near * TILE
    assert steps % TILE == 0 and rows == size == 2 * LANES and clusters * size == panels
    args = (
        residual, members, eig_vectors, eig_left, eig_values, compress,
        jnp.swapaxes(expand, 1, 2), neighbors, coupling,
    )
    carry = (clusters * sources, size)
    block = (2 * TILE, LANES)
    dma = pltpu.SemaphoreType.DMA
    return pl.pallas_call(
        kernel,
        out_shape=pltpu.VMEM(residual.shape, F32),
        in_specs=[pl.BlockSpec(memory_space=pltpu.HBM)] * len(args),
        out_specs=pl.BlockSpec(memory_space=pltpu.VMEM),
        scratch_shapes=[pltpu.VMEM(a.shape, a.dtype) for a in args]
        + [
            pltpu.VMEM((clusters, panels, size), BF16),
            pltpu.VMEM((near, TILE, panels), F32),
            pltpu.VMEM((near, TILE, panels), F32),
            pltpu.VMEM((rows, panels), F32),
            pltpu.VMEM(carry, F32),
            pltpu.VMEM((EXACT,) + carry, F32),
            pltpu.VMEM(block, BF16),
            pltpu.VMEM((times - 1 - EXACT,) + block, BF16),
            pltpu.VMEM((TILE, spaces * TILE), F32),
            pltpu.VMEM((near, TILE, spaces * TILE), F32),
            pltpu.VMEM((near,) + block, BF16),
            pltpu.VMEM((spaces,) + block, BF16),
            pltpu.VMEM((near, TILE, rows), F32),
            pltpu.VMEM((near, TILE, rows), F32),
            dma((len(args),)),
            pltpu.SemaphoreType.REGULAR,
            pltpu.SemaphoreType.REGULAR,
        ]
        + [dma(())] * 10,
        compiler_params=pltpu.CompilerParams(
            collective_id=0, has_side_effects=True, vmem_limit_bytes=32 * 1024 * 1024
        ),
    )(*(pltpu.with_memory_space_constraint(a, pltpu.HBM) for a in args))


def solution(mesh):
    return jax.shard_map(
        on_device,
        mesh=mesh,
        in_specs=(
            P(None, "tm", "space"),
            P("space", None),
            P("space", None, None),
            P("space", None, None),
            P("space", None),
            P("space", None, None),
            P("space", None, None),
            P("space", None),
            P("space", None),
        ),
        out_specs=P(None, "tm", "space"),
        check_vma=False,
    )
```

```python
import jax
import jax.numpy as jnp
from jax import lax
from jax.experimental import pallas as pl
from jax.experimental.pallas import tpu as pltpu
from jax.sharding import PartitionSpec as P

MESH = pl.DeviceIdType.MESH
F32, BF16 = jnp.float32, jnp.bfloat16
PLANES, CORES = 4, 2
EXACT = 4
RUN = 4
TILE, LANES = 8, 128


def dot(a, b, dims):
    return lax.dot_general(
        a, b, ((dims[:1], dims[1:]), ((), ())), preferred_element_type=F32
    )


def halves(a):
    high = a.astype(BF16)
    return high, (a - high.astype(F32)).astype(BF16)


def dot3(a, b, dims):
    return dot(a[0], b[0], dims) + (dot(a[0], b[1], dims) + dot(a[1], b[0], dims))


def kernel(
    x_hbm, members_hbm, v_hbm, w_hbm, lam_hbm, c_hbm, e_hbm, near_hbm, coup_hbm, out_ref,
    x_ref, members_ref, v_ref, w_ref, lam_ref, c_ref, e_ref, near_ref, coup_ref,
    place_ref, cv_ref, ep_ref, base_ref,
    ends, ends_in, short, short_in, sel_out, sel_in, sum_out, sum_in, mix_out, mix_in,
    load_sem, answer_sem, late_sem, ends_send, ends_recv, short_send, short_recv, sel_send, sel_recv, sum_send, sum_recv,
    mix_send, mix_recv,
):
    sources, steps, panels = x_ref.shape
    clusters, size = members_ref.shape
    rank = c_ref.shape[1]
    rows = sources * steps
    times, spaces = lax.axis_size("tm"), lax.axis_size("space")
    near = spaces // PLANES
    tm, space = lax.axis_index("tm"), lax.axis_index("space")
    plane = space // CORES % PLANES
    spot = space // (PLANES * CORES) * CORES + space % CORES
    per_block = rank // near

    def peer(at_plane, at_spot):
        return at_spot // CORES * (PLANES * CORES) + at_plane * CORES + at_spot % CORES

    def each(low, high, act):
        if isinstance(low, int) and isinstance(high, int):
            for i in range(low, high):
                act(i)
            return

        def body(i, _):
            act(i)
            return _

        lax.fori_loop(low, high, body, 0)

    def each_time(act):
        runs = times // RUN
        low = tm // RUN < runs // 2
        for i in range(runs):
            run = jnp.where(low, runs - 1 - i, i)
            for turn in sorted(range(RUN), key=lambda n: -min(n, RUN - n)):
                other = run * RUN + (tm + turn) % RUN
                if turn or (runs > 1 and i < runs // 2):
                    act(other)
                else:
                    pl.when(other != tm)(lambda other=other: act(other))

    def spots(first):
        return sorted(range(first, near), key=lambda n: min(n // CORES, (near - n) // CORES))

    far_first = sorted(range(near), key=lambda n: -min(n, near - n))

    def in_planes(*which):
        return pl.when(plane == which[0] if len(which) == 1 else plane % 2 == 1)

    barrier = pltpu.get_barrier_semaphore()

    def greet(device):
        pl.semaphore_signal(barrier, inc=1, device_id=device, device_id_type=MESH)

    @in_planes(2)
    def _():
        greet((tm, peer(1, spot)))
        greet((tm, peer(3, spot)))

    @in_planes(1, 3)
    def _():
        for k in spots(0):
            greet((tm, peer(0, (spot + k) % near)))

    @in_planes(0)
    def _():
        for k in spots(0):
            greet((tm, peer(2, (spot + k) % near)))

    each_time(lambda other: greet((other, space)))
    for k in spots(1):
        greet((tm, peer(plane, (spot + k) % near)))

    loads = [
        pltpu.make_async_copy(src, dst, load_sem.at[i])
        for i, (src, dst) in enumerate(
            (
                (members_hbm, members_ref),
                (x_hbm, x_ref),
                (w_hbm, w_ref),
                (lam_hbm, lam_ref),
                (v_hbm, v_ref),
                (c_hbm, c_ref),
                (e_hbm, e_ref),
                (near_hbm, near_ref),
                (coup_hbm, coup_ref),
            )
        )
    ]
    for load in loads:
        load.start()

    loads[0].wait()
    panel_ids = lax.broadcasted_iota(jnp.int32, (panels, size), 0) + space * panels
    for c in range(clusters):
        place_ref[c] = jnp.where(panel_ids == members_ref[c : c + 1, :], 1.0, 0.0).astype(BF16)

    loads[1].wait()
    x = halves(x_ref[...].reshape(rows, panels))
    ordered = [[dot(half, place_ref[c], (1, 0)).astype(BF16) for half in x] for c in range(clusters)]
    loads[2].wait()
    loads[3].wait()

    lam = jnp.concatenate(
        [jnp.broadcast_to(lam_ref[c : c + 1, :], (sources, size)) for c in range(clusters)], axis=0
    )
    power = {1: 1.0 / (1.0 + lam)}
    n = 1
    while n < steps * times:
        power[2 * n] = power[n] * power[n]
        n *= 2

    local = []
    for c in range(clusters):
        modes = dot3(ordered[c], halves(w_ref[c]), (1, 1))
        own = slice(c * sources, c * sources + 1)
        z = (modes * power[1][own]).reshape(rows // TILE, TILE, size)
        row = lax.broadcasted_iota(jnp.int32, (TILE, size), 0)
        ramp = power[1][own]
        for n in (1, 2, 4):
            z = z + jnp.where(row >= n, power[n][own], 0.0)[None] * pltpu.roll(z, n, 1)
            ramp = ramp * jnp.where(row // n % 2 == 1, power[n][own], 1.0)
        z = z.reshape(sources, steps // TILE, TILE, size)
        blocks = [z[:, 0]]
        for b in range(1, steps // TILE):
            blocks.append(z[:, b] + ramp[None] * blocks[-1][:, TILE - 1 :, :])
        local.append((blocks, ramp))
        ends[c * sources : (c + 1) * sources, :] = blocks[-1][:, TILE - 1, :]

    short[...] = jnp.concatenate(
        [ends[:, i : i + LANES] for i in range(0, size, LANES)], axis=0
    ).astype(BF16)

    far = jnp.where(plane == 0, 2 * near, jnp.where(plane == 2, near, 1))
    pl.semaphore_wait(barrier, times - 1 + near - 1 + far)

    def copy(src, dst, send, recv, device):
        return pltpu.make_async_remote_copy(
            src_ref=src, dst_ref=dst, send_sem=send, recv_sem=recv,
            device_id=device, device_id_type=MESH,
        )

    def answer(sem, to_plane):
        pl.semaphore_signal(
            sem, inc=1, device_id=(tm, peer(to_plane, spot)), device_id_type=MESH
        )

    @in_planes(0)
    def _():
        answer(answer_sem, 1)
        answer(answer_sem, 3)

    def send_ends(other):
        back = (other - tm + times) % times

        @pl.when(back > EXACT)
        def _():
            at = jnp.maximum(back - EXACT - 1, 0)
            copy(short, short_in.at[at], short_send, short_recv, (other, space)).start()

        @pl.when(back <= EXACT)
        def _():
            at = jnp.minimum(back - 1, EXACT - 1)
            copy(ends, ends_in.at[at], ends_send, ends_recv, (other, space)).start()

    each_time(send_ends)
    @in_planes(1, 3)
    def _():
        answer(answer_sem, 2)

    @in_planes(2)
    def _():
        answer(answer_sem, 0)

    for load in loads[4:]:
        load.wait()
    coupled = [
        jnp.concatenate(
            [jnp.broadcast_to(ref[c : c + 1, :], (per_block, ref.shape[1])) for c in range(clusters)],
            axis=0,
        )
        for ref in (near_ref, coup_ref)
    ]
    spread = (TILE, spaces * TILE)
    lane = lax.broadcasted_iota(jnp.int32, spread, 1)
    select = jnp.zeros(spread, F32)
    for n in range(near_ref.shape[1]):
        hit = coupled[0][:, n : n + 1] == lane // per_block
        select = select + jnp.where(hit, coupled[1][:, n : n + 1], 0.0)
    same = lane % per_block == lax.broadcasted_iota(jnp.int32, spread, 0) % per_block
    sel_out[...] = jnp.where(same, select, 0.0)
    sel_in[pl.ds(spot, 1)] = sel_out[...][None]

    cv_ref[...] = jnp.zeros_like(cv_ref)
    vectors = [halves(v_ref[c]) for c in range(clusters)]
    for c in range(clusters):
        at = slice(c * per_block, (c + 1) * per_block)
        cv = dot3(halves(c_ref[c]), vectors[c], (1, 0))
        spread_e = [dot(half, place_ref[c], (1, 1)) for half in halves(e_ref[c])]
        ep = spread_e[0] + spread_e[1]
        for b in range(near):
            block = slice(b * per_block, (b + 1) * per_block)
            cv_ref[b, at, c * size : (c + 1) * size] = cv[block]
            ep_ref[b, at, :] = ep[block]

    compress = halves(cv_ref[...].reshape(rank * clusters, panels))
    round_period = 1.0 / (1.0 - power[steps * times])
    pltpu.make_async_copy(short_in, short_in, short_recv).wait()
    pltpu.make_async_copy(ends_in, ends_in, ends_recv).wait()
    carry = ends[...]
    for k in range(times - 1, 0, -1):
        if k > EXACT:
            end = short_in[k - EXACT - 1].astype(F32)
            end = jnp.concatenate([end[i : i + TILE] for i in range(0, end.shape[0], TILE)], axis=1)
        else:
            end = ends_in[k - 1]
        carry = carry * power[steps] + end
    carry = carry * round_period

    solved = []
    for c in range(clusters):
        blocks, ramp = local[c]
        own = slice(c * sources, (c + 1) * sources)
        step = carry[own]
        parts = []
        for b in range(steps // TILE):
            parts.append(blocks[b] + ramp[None] * step[:, None, :])
            step = step * power[TILE][own]
        solved.append(halves(jnp.stack(parts, axis=1).reshape(rows, size)))
    summary = None
    for c in range(clusters):
        at = slice(c * size, (c + 1) * size)
        term = dot3([half[:, at] for half in compress], solved[c], (1, 1))
        summary = term if summary is None else summary + term
    summary = summary.reshape(near, TILE, rows)
    sum_out[...] = jnp.concatenate(
        [summary[:, :, i : i + LANES] for i in range(0, rows, LANES)], axis=1
    ).astype(BF16)

    def send_sum(to_plane, to_spots):
        for to in to_spots:
            copy(
                sum_out.at[to], sum_in.at[space], sum_send, sum_recv, (tm, peer(to_plane, to))
            ).start()

    def send_own():
        send_sum(plane, [(spot + k) % near for k in far_first if k])

    @in_planes(0)
    def _():
        send_own()
        send_sum(1, range(near))
        send_sum(3, range(near))
        pl.semaphore_wait(answer_sem, 1)
        send_sum(2, range(near))

    @in_planes(1, 3)
    def _():
        pl.semaphore_wait(answer_sem, 1)
        send_sum(0, [(spot + k) % near for k in far_first])
        send_own()
        send_sum(4 - plane, range(near))
        pl.semaphore_wait(late_sem, 1)
        send_sum(2, range(near))

    @in_planes(2)
    def _():
        send_sum(0, [(spot + k) % near for k in far_first])
        send_own()
        pl.semaphore_wait(answer_sem, 2)
        answer(late_sem, 1)
        answer(late_sem, 3)
        send_sum(1, range(near))
        send_sum(3, range(near))

    sum_in[pl.ds(space, 1)] = sum_out[pl.ds(spot, 1)]

    each(
        1, near,
        lambda k: copy(
            sel_out, sel_in.at[spot], sel_send, sel_recv, (tm, peer(plane, (spot + k) % near))
        ).start(),
    )
    base = None
    for c in range(clusters):
        for half in halves(dot3(solved[c], vectors[c], (1, 1))):
            term = dot(half, place_ref[c], (1, 1))
            base = term if base is None else base + term
    base_ref[...] = base
    expand = halves(-ep_ref[...].reshape(rank * clusters, panels))
    expand = jnp.concatenate([expand[0], expand[1], expand[0]], axis=0)

    plane_peers = pl.ds(0, near - 1)
    pltpu.make_async_copy(sel_in.at[plane_peers], sel_in.at[plane_peers], sel_recv).wait()
    selector = halves(sel_in[...].reshape(near * TILE, spaces * TILE))
    everyone = pl.ds(0, spaces - 1)
    pltpu.make_async_copy(sum_in.at[everyone], sum_in.at[everyone], sum_recv).wait()
    gathered = sum_in[...].astype(F32)
    for i in range(rows // LANES):
        part = gathered[:, i * TILE : (i + 1) * TILE, :].reshape(spaces * TILE, LANES).astype(BF16)
        mixed = dot(selector[0], part, (1, 0)) + dot(selector[1], part, (1, 0))
        mix_out[:, :, i * LANES : (i + 1) * LANES] = mixed.reshape(near, TILE, LANES)

    def send_mix(to):
        copy(mix_out.at[to], mix_in.at[spot], mix_send, mix_recv, (tm, peer(plane, to))).start()

    for k in far_first:
        if k:
            send_mix((spot + k) % near)
    mix_in[pl.ds(spot, 1)] = mix_out[pl.ds(spot, 1)]
    pltpu.make_async_copy(mix_in.at[plane_peers], mix_in.at[plane_peers], mix_recv).wait()

    mixed = halves(mix_in[...].reshape(rank * clusters, rows))
    mixed = jnp.concatenate([mixed[0], mixed[0], mixed[1]], axis=0)
    out_ref[...] = (base_ref[...] + dot(mixed, expand, (0, 0))).reshape(out_ref.shape)

    pltpu.make_async_copy(short_in, short_in, short_send).wait()
    pltpu.make_async_copy(ends_in, ends_in, ends_send).wait()
    pltpu.make_async_copy(sel_in.at[plane_peers], sel_in.at[plane_peers], sel_send).wait()
    pltpu.make_async_copy(sum_in.at[everyone], sum_in.at[everyone], sum_send).wait()
    pltpu.make_async_copy(mix_in.at[plane_peers], mix_in.at[plane_peers], mix_send).wait()


def on_device(
    residual, members, eig_vectors, eig_left, eig_values, compress, expand, neighbors, coupling
):
    sources, steps, panels = residual.shape
    clusters, size = members.shape
    rank = compress.shape[1]
    rows = sources * steps
    times, spaces = lax.axis_size("tm"), lax.axis_size("space")
    near = spaces // PLANES
    assert clusters * sources == TILE and clusters * rank == near * TILE
    assert steps % TILE == 0 and rows == size == 2 * LANES and clusters * size == panels
    args = (
        residual, members, eig_vectors, eig_left, eig_values, compress,
        jnp.swapaxes(expand, 1, 2), neighbors, coupling,
    )
    carry = (clusters * sources, size)
    block = (2 * TILE, LANES)
    dma = pltpu.SemaphoreType.DMA
    return pl.pallas_call(
        kernel,
        out_shape=pltpu.VMEM(residual.shape, F32),
        in_specs=[pl.BlockSpec(memory_space=pltpu.HBM)] * len(args),
        out_specs=pl.BlockSpec(memory_space=pltpu.VMEM),
        scratch_shapes=[pltpu.VMEM(a.shape, a.dtype) for a in args]
        + [
            pltpu.VMEM((clusters, panels, size), BF16),
            pltpu.VMEM((near, TILE, panels), F32),
            pltpu.VMEM((near, TILE, panels), F32),
            pltpu.VMEM((rows, panels), F32),
            pltpu.VMEM(carry, F32),
            pltpu.VMEM((EXACT,) + carry, F32),
            pltpu.VMEM(block, BF16),
            pltpu.VMEM((times - 1 - EXACT,) + block, BF16),
            pltpu.VMEM((TILE, spaces * TILE), F32),
            pltpu.VMEM((near, TILE, spaces * TILE), F32),
            pltpu.VMEM((near,) + block, BF16),
            pltpu.VMEM((spaces,) + block, BF16),
            pltpu.VMEM((near, TILE, rows), F32),
            pltpu.VMEM((near, TILE, rows), F32),
            dma((len(args),)),
            pltpu.SemaphoreType.REGULAR,
            pltpu.SemaphoreType.REGULAR,
        ]
        + [dma(())] * 10,
        compiler_params=pltpu.CompilerParams(
            collective_id=0, has_side_effects=True, vmem_limit_bytes=32 * 1024 * 1024
        ),
    )(*(pltpu.with_memory_space_constraint(a, pltpu.HBM) for a in args))


def solution(mesh):
    return jax.shard_map(
        on_device,
        mesh=mesh,
        in_specs=(
            P(None, "tm", "space"),
            P("space", None),
            P("space", None, None),
            P("space", None, None),
            P("space", None),
            P("space", None, None),
            P("space", None, None),
            P("space", None),
            P("space", None),
        ),
        out_specs=P(None, "tm", "space"),
        check_vma=False,
    )
```
